256 devices in a mesh: wide: 32 (over z, x), narrow: 8 (over y, core).
Axes of the slice: x: 4, y: 4, z: 8, core: 2. Of those that a mesh axis runs over, the one named last changes fastest.
Arguments:
- initial: float32 [64, 512, 8192], P(None, 'wide', 'narrow'), may hold values from -50 to 50, as said below
- kappa: float32 [4, 512, 8192], P(None, 'wide', 'narrow'), may hold values from 0.3 to 1.2
- decay: float32 [512, 8192], P('wide', 'narrow'), may hold values from 0.05 to 0.5
- field_index: int32 [64], replicated, may hold values from 0 to 3
Outputs:
- basis: float32 [128, 512, 8192], P(None, 'wide', 'narrow')
- triangle: float32 [128, 128], replicated
The draws below stay inside these ranges and needn't reach their ends.
Inputs may be any that keep to these rules, and one draw needn't show every extreme that they name: Every value of every sample's initial field lies in this range.
All inputs are finite; a program needn't handle non-finite values.
Results may differ from the reference program's by a relative error of at most 0.0003.
Values sent between devices are 32-bit elements; how exact they have to be, the bound alone decides.
No kernel may reach another device: no remote copies, remote signals or barrier semaphores. Data moves between devices by JAX's collectives and lax.ppermute only.
A program may use at most 128 MiB of HBM per device.

```python
import math
import jax
import jax.numpy as jnp

SAMPLES = 64
NCOEF = 4
CX = 16
SNAPS = 128
NX = 512
NY = 8192


def draw_initial(key, part):
    base_key = jax.random.fold_in(key, 7)
    k_base, k_jitter, k_column = jax.random.split(base_key, 3)
    row_pos = jnp.arange(NX).astype(jnp.float32) / float(NX)
    col_pos = jnp.arange(NY).astype(jnp.float32) / float(NY)
    jitter = jax.random.uniform(k_jitter, (NX, NY), jnp.float32)
    amplitude = 10.0 ** (0.5 * row_pos[:, None] + 0.5 * col_pos[None, :] + 0.3 * jitter - 0.8)
    column = 10.0 ** jax.random.uniform(k_column, (SAMPLES, 1, 1), jnp.float32, -0.5, 0.5)
    values = jnp.clip(jax.random.normal(k_base, (SAMPLES, NX, NY), jnp.float32), -5.0, 5.0)
    return (column * amplitude * values).astype(jnp.float32)


def place_ends(array, stream_key, least, top_value):
    longest = array.shape.index(max(array.shape))
    spots = []
    for shift in (0, 1):
        where = [jax.random.randint(jax.random.fold_in(stream_key, axis), (), 0, length) for axis, length in enumerate(array.shape)]
        where[longest] = (where[longest] + shift) % array.shape[longest]
        spots.append(tuple(where))
    return array.at[spots[0]].set(least).at[spots[1]].set(top_value)


def shard_levels(key, dims, shards, smallest, largest):
    factor_of = 1.0
    for dim, blocks in shards:
        draws = jax.random.uniform(jax.random.fold_in(jax.random.fold_in(key, 6), dim), (blocks,), jnp.float32, smallest / len(shards), largest / len(shards))
        factor_of = factor_of * jnp.repeat(jnp.exp(draws), dims[dim] // blocks).reshape((-1,) + (1,) * (len(dims) - 1 - dim))
    return factor_of


def setup_inputs(seed: int = 0) -> dict:
    streams_of = jax.random.split(jax.random.key(seed), 5)
    return {
        "initial": draw_initial(jax.random.fold_in(streams_of[4], 71), 0),
        "kappa": jnp.clip(0.3 + 0.90000004 * jax.random.uniform(streams_of[1], (NCOEF, NX, NY), jnp.float32) ** shard_levels(streams_of[1], (NCOEF, NX, NY), ((1, 32), (2, 8)), -0.2, 0.2), 0.3, 1.2),
        "decay": jnp.clip(jnp.exp(math.log(0.5) - 2.3025851 * jax.random.uniform(streams_of[2], (NX, NY), jnp.float32) ** shard_levels(streams_of[2], (NX, NY), ((0, 32), (1, 8)), -0.2, 0.2)), 0.05, 0.5),
        "field_index": place_ends(jax.random.randint(streams_of[3], (SAMPLES,), 0, NCOEF), jax.random.fold_in(streams_of[3], 1), 0, NCOEF - 1).astype(jnp.int32),
    }


def advance(state, coefficient, decay):
    padded = jnp.pad(state, ((0, 0), (1, 1), (1, 1)))
    neighbours = padded[:, 2:, 1:-1] + padded[:, :-2, 1:-1] + padded[:, 1:-1, 2:] + padded[:, 1:-1, :-2]
    return state + 0.2 * coefficient * (neighbours - 4.0 * state) - decay * state

def reference(initial, kappa, decay, field_index):
    coefficient = kappa[field_index]
    first = advance(initial, coefficient, decay)
    second = advance(first, coefficient, decay)
    snapshots = jnp.concatenate([first, second], 0).reshape(SNAPS, NX * NY)
    slab_cells = CX * NY
    factors = []
    for slab in range(NX // CX):
        block = snapshots[:, slab * slab_cells:(slab + 1) * slab_cells]
        factors.append(jnp.linalg.qr(block.T, mode='r'))
    stacked = jnp.concatenate(factors, 0)
    rfactor = jnp.linalg.qr(stacked, mode='r')
    signs = jnp.sign(jnp.diagonal(rfactor))
    rfactor = rfactor * signs[:, None]
    basis_rows = jax.scipy.linalg.solve_triangular(rfactor.T, snapshots, lower=True)
    scale = (NX * NY) ** 0.5
    basis = (basis_rows * scale).reshape(SNAPS, NX, NY)
    return (basis, rfactor / scale)
```

```python
import math

import jax
import jax.numpy as jnp
from jax import lax
from jax.experimental import pallas as pl
from jax.experimental.pallas import tpu as pltpu
from jax.sharding import Mesh, PartitionSpec as P

F32, BF16 = jnp.float32, jnp.bfloat16
S, ROWS, COLS, FIELDS = 64, 16, 1024, 4
SNAP = 2 * S
TILES, GROUPS = COLS // 128, S // 8
EXT = S + 8
KAP, DEC = S, S + FIELDS
BLOCK = 16
ROWAXIS, COLAXIS = ("z", "x"), ("y", "core")
ANY = pl.BlockSpec(memory_space=pl.ANY)
VM = pl.BlockSpec(memory_space=pltpu.VMEM)
VMEM_LIMIT = 24 * 2**20


def params():
    return pltpu.CompilerParams(vmem_limit_bytes=VMEM_LIMIT)


def lanes():
    return lax.broadcasted_iota(jnp.int32, (8, 128), 1)


def tile(t):
    return slice(128 * t, 128 * t + 128)


def group(g):
    return slice(8 * g, 8 * g + 8)


def pack_kernel(u, kap, dec, uall, north, south, west, east, sems):
    for x in range(ROWS):
        uall[x, S:EXT, :] = jnp.zeros((8, COLS), F32)
    order = [0, ROWS - 1] + list(range(1, ROWS - 1))
    copies = {}
    for x in order:
        copies[x] = (
            pltpu.make_async_copy(u.at[:, x, :], uall.at[x, 0:S, :], sems.at[0, x]),
            pltpu.make_async_copy(kap.at[:, x, :], uall.at[x, KAP : KAP + FIELDS, :], sems.at[1, x]),
            pltpu.make_async_copy(dec.at[x : x + 1, :], uall.at[x, DEC : DEC + 1, :], sems.at[2, x]),
        )
        for copy in copies[x]:
            copy.start()
    lane = lanes()
    w = [jnp.zeros((8, 128), F32) for _ in range(GROUPS + 1)]
    e = [jnp.zeros((8, 128), F32) for _ in range(GROUPS + 1)]
    for x in order:
        for copy in copies[x]:
            copy.wait()
        if x == 0:
            north[...] = uall[0]
        if x == ROWS - 1:
            south[...] = uall[ROWS - 1]
        for g in range(GROUPS + 1):
            first, last = uall[x, group(g), tile(0)], uall[x, group(g), tile(TILES - 1)]
            w[g] = jnp.where(lane == x, pltpu.roll(first, x, 1), w[g])
            w[g] = jnp.where(lane == ROWS + x, pltpu.roll(first, ROWS + x - 1, 1), w[g])
            e[g] = jnp.where(lane == x, pltpu.roll(last, x + 1, 1), e[g])
            e[g] = jnp.where(lane == ROWS + x, pltpu.roll(last, ROWS + x + 2, 1), e[g])
    for g in range(GROUPS + 1):
        west[group(g), :] = w[g]
        east[group(g), :] = e[g]


def pack(initial, kappa, decay):
    row, col = pltpu.VMEM((EXT, COLS), F32), pltpu.VMEM((EXT, 128), F32)
    return pl.pallas_call(
        pack_kernel,
        name="pack",
        in_specs=[ANY] * 3,
        out_specs=[VM] * 5,
        out_shape=[pltpu.VMEM((ROWS, EXT, COLS), F32), row, row, col, col],
        scratch_shapes=[pltpu.SemaphoreType.DMA((3, ROWS))],
        compiler_params=params(),
    )(initial, kappa, decay)


def field_rows(load, t):
    k = [jnp.broadcast_to(load(KAP + c, t), (8, 128)) * 0.2 for c in range(FIELDS)]
    return k, 1.0 - jnp.broadcast_to(load(DEC, t), (8, 128))


def choose(k, f):
    odd = (f & 1) == 1
    return jnp.where((f & 2) == 2, jnp.where(odd, k[3], k[2]), jnp.where(odd, k[1], k[0]))


def step_row(fi, load_field, center, above, below, edge_w, edge_e, emit):
    lane = lanes()
    low, high = lane == 0, lane == 127
    from_w = [edge_w(g) for g in range(GROUPS)]
    from_e = [pltpu.roll(center(g, 0), 127, 1) for g in range(GROUPS)]
    for t in range(TILES):
        k, keep = field_rows(load_field, t)
        held = None
        for g in range(GROUPS):
            here = center(g, t)
            right = pltpu.roll(here, 1, 1)
            west = jnp.where(low, from_w[g], right)
            from_w[g] = right
            nxt = pltpu.roll(center(g, t + 1), 127, 1) if t + 1 < TILES else edge_e(g)
            east = jnp.where(high, nxt, from_e[g])
            from_e[g] = nxt
            b = choose(k, fi[group(g), :])
            a = keep - 4.0 * b
            new = a * here + b * ((above(g, t) + below(g, t)) + (west + east))
            if g % 2 == 0:
                held = new
            else:
                emit(g - 1, t, held, new)


def split_store(hi, lo, index, base, g, t, first, second):
    both = jnp.concatenate([first, second], 0)
    top = both.astype(BF16)
    rest = (both - top.astype(F32)).astype(BF16)
    where = slice(base + 8 * g, base + 8 * g + 16)
    hi[index, where, tile(t)] = top
    lo[index, where, tile(t)] = rest


def gram(acc, hi, lo):
    rhs = jnp.concatenate([hi, lo], 0)
    acc[...] += lax.dot_general(hi, rhs, (((1,), (1,)), ((), ())), preferred_element_type=F32)


def column_step(fi, halo, own, g, up=None, down=None):
    lane = lanes()
    one = halo[group(g), :]
    two = pltpu.roll(one, 128 - ROWS, 1)
    k = [jnp.broadcast_to(halo[KAP + c : KAP + c + 1, :], (8, 128)) * 0.2 for c in range(FIELDS)]
    keep = 1.0 - jnp.broadcast_to(halo[DEC : DEC + 1, :], (8, 128))
    b = choose(k, fi[group(g), :])
    above, below = pltpu.roll(one, 1, 1), pltpu.roll(one, 127, 1)
    if up is not None:
        above = jnp.where(lane == 0, up, above)
        below = jnp.where(lane == ROWS - 1, down, below)
    return (keep - 4.0 * b) * one + b * ((above + below) + (two + own[group(g), :]))


def interior_kernel(fi, uall, own_w, own_e, halo_w, halo_e, first, hi, lo, acc, col_w, col_e):
    acc[...] = jnp.zeros_like(acc)
    for g in range(GROUPS):
        col_w[group(g), :] = column_step(fi, halo_w, own_w, g)
        col_e[group(g), :] = column_step(fi, halo_e, own_e, g)

    def field(x):
        return lambda r, t: uall[x, r : r + 1, tile(t)]

    def one(x, keep):
        def emit(g, t, p, q):
            first[x, group(g), tile(t)] = p
            first[x, group(g + 1), tile(t)] = q
            if keep:
                split_store(hi, lo, x - 2, 0, g, t, p, q)

        step_row(
            fi,
            field(x),
            lambda g, t: uall[x, group(g), tile(t)],
            lambda g, t: uall[x - 1, group(g), tile(t)],
            lambda g, t: uall[x + 1, group(g), tile(t)],
            lambda g: pltpu.roll(halo_w[group(g), :], (128 - x) % 128, 1),
            lambda g: pltpu.roll(halo_e[group(g), :], 127 - x, 1),
            emit,
        )

    def two(x):
        step_row(
            fi,
            field(x),
            lambda g, t: first[x, group(g), tile(t)],
            lambda g, t: first[x - 1, group(g), tile(t)],
            lambda g, t: first[x + 1, group(g), tile(t)],
            lambda g: pltpu.roll(col_w[group(g), :], (128 - x) % 128, 1),
            lambda g: pltpu.roll(col_e[group(g), :], 127 - x, 1),
            lambda g, t, p, q: split_store(hi, lo, x - 2, S, g, t, p, q),
        )

    one(1, False)
    one(2, True)

    def body(x, carry):
        one(x, True)
        two(x - 1)
        gram(acc, hi[x - 3], lo[x - 3])
        return carry

    lax.fori_loop(3, ROWS - 2, body, 0)
    one(ROWS - 2, False)
    two(ROWS - 3)
    gram(acc, hi[ROWS - 5], lo[ROWS - 5])


def interior(fi, uall, own_w, own_e, halo_w, halo_e):
    snap = pltpu.VMEM((ROWS - 4, SNAP, COLS), BF16)
    return pl.pallas_call(
        interior_kernel,
        name="interior",
        in_specs=[VM] * 6,
        out_specs=[VM] * 4,
        out_shape=[pltpu.VMEM((ROWS, S, COLS), F32), snap, snap, pltpu.VMEM((SNAP, 2 * SNAP), F32)],
        scratch_shapes=[pltpu.VMEM((S, 128), F32)] * 2,
        cost_estimate=pl.CostEstimate(flops=2 * 12 * SNAP * 2 * SNAP * COLS, bytes_accessed=2**25, transcendentals=0),
        compiler_params=params(),
    )(fi, uall, own_w, own_e, halo_w, halo_e)


def edge_kernel(
    fi, uall, own_w, own_e, halo_w, halo_e, first, inner, n1, s1, n2, s2, hi, lo, packed, col_w, col_e, edge, acc
):
    acc[...] = inner[...]
    lane = lanes()
    corner = slice(COLS, COLS + 128)
    for g in range(GROUPS):
        up, down = n2[group(g), corner], s2[group(g), corner]
        col_w[group(g), :] = column_step(fi, halo_w, own_w, g, up, pltpu.roll(down, ROWS - 1, 1))
        col_e[group(g), :] = column_step(fi, halo_e, own_e, g, pltpu.roll(up, 127, 1), pltpu.roll(down, ROWS - 2, 1))

    def rows(ref):
        return lambda g, t: ref[group(g), tile(t)]

    def at(ref, x):
        return lambda g, t: ref[x, group(g), tile(t)]

    def field(x):
        return lambda r, t: uall[x, r : r + 1, tile(t)]

    def pick(ref, x, to):
        return lambda g: pltpu.roll(ref[group(g), :], (to - x) % 128, 1)

    last = ROWS - 1
    for near, far, row, inside, slot, beyond in ((n1, n2, 0, 1, 0, 2), (s1, s2, last, last - 1, 2, 3)):

        def put(index):
            def emit(g, t, p, q):
                edge[index, group(g), tile(t)] = p
                edge[index, group(g + 1), tile(t)] = q

            return emit

        def put_both(index, target):
            def emit(g, t, p, q):
                put(index)(g, t, p, q)
                split_store(hi, lo, target, 0, g, t, p, q)

            return emit

        def put_second(target):
            return lambda g, t, p, q: split_store(hi, lo, target, S, g, t, p, q)

        outer = 0 if row == 0 else 3
        inner_slot = 1 if row == 0 else 2
        step_row(
            fi,
            lambda r, t, near=near: near[r : r + 1, tile(t)],
            rows(near),
            rows(far),
            at(uall, row),
            pick(far_corner(far), 0, 0),
            pick(far_corner(far), 1, 127),
            put(0),
        )
        step_row(
            fi, field(row), at(uall, row), rows(near), at(uall, inside),
            pick(halo_w, row, 0), pick(halo_e, row, 127), put_both(1, outer),
        )
        step_row(
            fi, field(row), at(edge, 1), at(edge, 0), at(first, inside),
            pick(col_w, row, 0), pick(col_e, row, 127), put_second(outer),
        )
        deeper = inside + (inside - row)
        step_row(
            fi, field(inside), at(first, inside), at(edge, 1), at(first, deeper),
            pick(col_w, inside, 0), pick(col_e, inside, 127), put_second(inner_slot),
        )
        for t in range(TILES):
            for g in range(0, GROUPS, 2):
                split_store(
                    hi, lo, inner_slot, 0, g, t,
                    first[inside, group(g), tile(t)], first[inside, group(g + 1), tile(t)],
                )
        gram(acc, hi[outer], lo[outer])
        gram(acc, hi[inner_slot], lo[inner_slot])
    cross = acc[:, SNAP:]
    full = acc[:, :SNAP] + (cross + cross.T)
    top, bottom = full[:S, :], pltpu.roll(full[S:, :], S, 1)
    r = lax.broadcasted_iota(jnp.int32, (S, SNAP), 0)
    c = lax.broadcasted_iota(jnp.int32, (S, SNAP), 1)
    packed[0:S, :] = jnp.where((c < S) & (r > c), bottom, top)
    diag = jnp.sum(jnp.where(r == c, bottom, 0.0), axis=0, keepdims=True)
    packed[S : S + 8, :] = jnp.where(lax.broadcasted_iota(jnp.int32, (8, SNAP), 0) == 0, diag, 0.0)
    packed[S + 8 :, :] = jnp.zeros((8, SNAP), F32)


def far_corner(ref):
    return ref.at[:, COLS : COLS + 128]


def edges(fi, uall, own_w, own_e, halo_w, halo_e, first, inner, n1, s1, n2, s2):
    snap = pltpu.VMEM((4, SNAP, COLS), BF16)
    return pl.pallas_call(
        edge_kernel,
        name="edges",
        in_specs=[VM] * 12,
        out_specs=[VM] * 3,
        out_shape=[snap, snap, pltpu.VMEM((S + 16, SNAP), F32)],
        scratch_shapes=[
            pltpu.VMEM((S, 128), F32),
            pltpu.VMEM((S, 128), F32),
            pltpu.VMEM((2, S, COLS), F32),
            pltpu.VMEM((SNAP, 2 * SNAP), F32),
        ],
        compiler_params=params(),
    )(fi, uall, own_w, own_e, halo_w, halo_e, first, inner, n1, s1, n2, s2)


def unpack(packed):
    top, diag = packed[0:S, :], packed[S : S + 1, :]
    r = lax.broadcasted_iota(jnp.int32, (S, SNAP), 0)
    c = lax.broadcasted_iota(jnp.int32, (S, SNAP), 1)
    upper = jnp.where(r <= c, top, 0.0)
    lower = pltpu.roll(jnp.where((r > c) & (c < S), top, 0.0), S, 1)
    on_diag = jnp.where(r == c - S, pltpu.roll(jnp.broadcast_to(diag, (8, SNAP)), S, 1)[0:1, :], 0.0)
    zero = jnp.zeros_like(lower)
    return jnp.concatenate([upper, on_diag], 0) + jnp.concatenate([zero, lower], 0).T


def factor(m, z):
    sub = lax.broadcasted_iota(jnp.int32, (8, 128), 0)
    for k in range(SNAP // BLOCK):
        lo = k * BLOCK
        panel = m[lo : lo + BLOCK, :]
        p = {}
        for i in range(BLOCK):
            for j in range(i, BLOCK):
                p[i, j] = jnp.broadcast_to(panel[i : i + 1, lo + j : lo + j + 1], (8, 128))
        rows = [[jnp.broadcast_to(panel[i : i + 1, tile(h)], (8, 128)) for h in range(2)] for i in range(BLOCK)]
        for j in range(BLOCK):
            r = lax.rsqrt(p[j, j])
            u = {i: p[j, i] * r for i in range(j + 1, BLOCK)}
            for i in range(j + 1, BLOCK):
                for l in range(i, BLOCK):
                    p[i, l] = p[i, l] - u[i] * u[l]
            rows[j] = [v * r for v in rows[j]]
            for i in range(j + 1, BLOCK):
                rows[i] = [v - u[i] * w for v, w in zip(rows[i], rows[j])]
        for part in range(BLOCK // 8):
            for h in range(2):
                v = rows[8 * part][h]
                for i in range(1, 8):
                    v = jnp.where(sub == i, rows[8 * part + i][h], v)
                z[lo + 8 * part : lo + 8 * part + 8, tile(h)] = v
        if lo + BLOCK < SNAP:
            done = z[lo : lo + BLOCK, :]
            update = lax.dot_general(
                done[:, :SNAP], done, (((0,), (0,)), ((), ())),
                precision=lax.Precision.HIGHEST, preferred_element_type=F32,
            )
            m[lo + BLOCK :, :] = m[lo + BLOCK :, :] - update[lo + BLOCK :, :]


def basis_kernel(scale, packed, hi, lo, ehi, elo, out, tri, m, z, buf, sems):
    r = lax.broadcasted_iota(jnp.int32, (SNAP, SNAP), 0)
    c = lax.broadcasted_iota(jnp.int32, (SNAP, SNAP), 1)
    m[:, :SNAP] = unpack(packed)
    m[:, SNAP:] = jnp.where(r == c, 1.0, 0.0)
    factor(m, z)
    tri[...] = jnp.where(r <= c, z[:, :SNAP], 0.0) * (1.0 / scale)
    w = jnp.where(r >= c, z[:, SNAP:], 0.0) * scale
    top = w.astype(BF16)
    rest = (w - top.astype(F32)).astype(BF16)
    lhs = jnp.concatenate([jnp.concatenate([top, top], 1), jnp.concatenate([rest, rest], 1)], 0)

    def copy(x):
        return pltpu.make_async_copy(buf.at[x], out.at[:, x, :], sems.at[x])

    def row(x, h, l):
        both = jnp.dot(lhs, jnp.concatenate([h, l], 0), preferred_element_type=F32)
        buf[x] = both[:SNAP] + both[SNAP:]
        copy(x).start()

    def body(i, carry):
        row(i + 2, hi[i], lo[i])
        return carry

    lax.fori_loop(0, ROWS - 4, body, 0)
    for i, x in enumerate((0, 1, ROWS - 2, ROWS - 1)):
        row(x, ehi[i], elo[i])
    for x in range(ROWS):
        copy(x).wait()


def make_basis(scale, packed, hi, lo, ehi, elo):
    def kernel(*refs):
        basis_kernel(scale, *refs)

    return pl.pallas_call(
        kernel,
        name="basis",
        in_specs=[VM] * 5,
        out_specs=[ANY, VM],
        out_shape=[
            jax.ShapeDtypeStruct((SNAP, ROWS, COLS), F32),
            jax.ShapeDtypeStruct((SNAP, SNAP), F32),
        ],
        scratch_shapes=[
            pltpu.VMEM((SNAP, 2 * SNAP), F32),
            pltpu.VMEM((SNAP, 2 * SNAP), F32),
            pltpu.VMEM((ROWS, SNAP, COLS), F32),
            pltpu.SemaphoreType.DMA((ROWS,)),
        ],
        compiler_params=params(),
    )(packed, hi, lo, ehi, elo)


def spread_sum(value, axis):
    count = lax.axis_size(axis)
    return lax.all_to_all(jnp.broadcast_to(value[None], (count, *value.shape)), axis, 0, 0).sum(0)


def sum_over_devices(packed):
    swap = [(0, 1), (1, 0)]
    second = lax.axis_index("core") == 1
    half = packed.shape[0] // 2
    a, b = packed[:half], packed[half:]
    mine = jnp.where(second, b, a) + lax.ppermute(jnp.where(second, a, b), "core", swap)
    mine = spread_sum(mine, ("x", "y"))
    mine = spread_sum(mine, "z")
    other = lax.ppermute(mine, "core", swap)
    return jnp.concatenate([jnp.where(second, other, mine), jnp.where(second, mine, other)], 0)


def along(axis):
    count = lax.axis_size(axis)
    return [(i, i + 1) for i in range(count - 1)], [(i + 1, i) for i in range(count - 1)]


def shards(initial, kappa, decay, field_index):
    fi = jnp.broadcast_to(field_index[:, None], (S, 128))
    uall, north, south, own_w, own_e = pack(initial, kappa, decay)
    up, down = along(ROWAXIS), along(COLAXIS)
    halo_w = lax.ppermute(own_e, COLAXIS, down[0])
    halo_e = lax.ppermute(own_w, COLAXIS, down[1])
    n1 = lax.ppermute(south, ROWAXIS, up[0])
    s1 = lax.ppermute(north, ROWAXIS, up[1])

    def far(row, edge_row):
        pad = jnp.zeros((S, 126), F32)
        ends = [h[:S, edge_row : edge_row + 1] for h in (halo_w, halo_e)]
        return jnp.concatenate([uall[row, :S, :], *ends, pad], 1)

    n2 = lax.ppermute(far(ROWS - 2, ROWS - 1), ROWAXIS, up[0])
    s2 = lax.ppermute(far(1, 0), ROWAXIS, up[1])
    first, hi, lo, inner = interior(fi, uall, own_w, own_e, halo_w, halo_e)
    ehi, elo, packed = edges(fi, uall, own_w, own_e, halo_w, halo_e, first, inner, n1, s1, n2, s2)
    total = sum_over_devices(packed)
    cells = lax.axis_size(ROWAXIS) * lax.axis_size(COLAXIS) * ROWS * COLS
    return make_basis(math.sqrt(cells), total, hi, lo, ehi, elo)


def solution(mesh):
    wide, narrow = mesh.devices.shape
    fine = Mesh(mesh.devices.reshape(wide // 4, 4, narrow // 2, 2), ("z", "x", "y", "core"))
    grid = P(None, ROWAXIS, COLAXIS)
    return jax.shard_map(
        shards,
        mesh=fine,
        in_specs=(grid, grid, P(ROWAXIS, COLAXIS), P()),
        out_specs=(grid, P()),
        check_vma=False,
    )
```

```python
import math

import jax
import jax.numpy as jnp
from jax import lax
from jax.experimental import pallas as pl
from jax.experimental.pallas import tpu as pltpu
from jax.sharding import Mesh, PartitionSpec as P

F32, BF16 = jnp.float32, jnp.bfloat16
S, ROWS, COLS, FIELDS = 64, 16, 1024, 4
SNAP = 2 * S
TILES, GROUPS = COLS // 128, S // 8
EXT = S + 8
KAP, DEC = S, S + FIELDS
HALF = (S + 16) // 2
THIRD = (ROWS - 4) // 3
BLOCK = 16
ROWAXIS, COLAXIS = ("z", "x"), ("y", "core")
FIELD, MESSAGE = 2 * COLS, 2 * COLS + 128
HBM = pl.BlockSpec(memory_space=pltpu.HBM)
VM = pl.BlockSpec(memory_space=pltpu.VMEM)


def params(mib):
    return pltpu.CompilerParams(vmem_limit_bytes=mib * 2**20)


def lanes():
    return lax.broadcasted_iota(jnp.int32, (8, 128), 1)


def tile(t):
    return slice(128 * t, 128 * t + 128)


def group(g):
    return slice(8 * g, 8 * g + 8)


def odd_row_device():
    return (lax.axis_index("x") & 1) == 1


def odd_column_device():
    return lax.axis_index("core") == 1


def row_kernel(u, kap, dec, first_to, second_to, usem, ksem):
    def send(order):
        copies = []
        for h, (to, near, far) in enumerate(order):
            copies.append(pltpu.make_async_copy(u.at[:, near, :], to.at[:, 0:COLS], usem.at[h, 0]))
            copies.append(pltpu.make_async_copy(u.at[:, far, :], to.at[:, COLS : 2 * COLS], usem.at[h, 1]))
        for copy in copies:
            copy.start()
        small = []
        for h, (to, near, _) in enumerate(order):
            to[:, FIELD : FIELD + 128] = jnp.zeros((S, 128), F32)
            for t in range(TILES):
                tiles = to.at[8 * t : 8 * t + FIELDS, FIELD : FIELD + 128]
                small.append(pltpu.make_async_copy(kap.at[:, near, tile(t)], tiles, ksem.at[h, 0, t]))
                line = to.at[8 * t + FIELDS : 8 * t + FIELDS + 1, FIELD : FIELD + 128]
                small.append(pltpu.make_async_copy(dec.at[near : near + 1, tile(t)], line, ksem.at[h, 1, t]))
        for copy in small:
            copy.start()
        for copy in copies + small:
            copy.wait()

    odd = odd_row_device()
    top, bottom = (0, 1), (ROWS - 1, ROWS - 2)

    @pl.when(odd)
    def _():
        send(((first_to, *top), (second_to, *bottom)))

    @pl.when(jnp.logical_not(odd))
    def _():
        send(((first_to, *bottom), (second_to, *top)))


def rows(initial, kappa, decay):
    message = pltpu.VMEM((S, MESSAGE), F32)
    return pl.pallas_call(
        row_kernel,
        name="rows",
        in_specs=[HBM] * 3,
        out_specs=[VM] * 2,
        out_shape=[message, message],
        scratch_shapes=[pltpu.SemaphoreType.DMA((2, 2)), pltpu.SemaphoreType.DMA((2, 2, TILES))],
        compiler_params=params(58),
    )(initial, kappa, decay)


def column_kernel(u, kap, dec, uall, west, east, first_to, second_to, sems):
    for x in range(ROWS):
        uall[x, S:EXT, :] = jnp.zeros((8, COLS), F32)
    copies = []
    for x in range(ROWS):
        copies.append(
            (
                pltpu.make_async_copy(u.at[:, x, :], uall.at[x, 0:S, :], sems.at[0, x]),
                pltpu.make_async_copy(kap.at[:, x, :], uall.at[x, KAP : KAP + FIELDS, :], sems.at[1, x]),
                pltpu.make_async_copy(dec.at[x : x + 1, :], uall.at[x, DEC : DEC + 1, :], sems.at[2, x]),
            )
        )
        for copy in copies[x]:
            copy.start()
    lane = lanes()
    w = [jnp.zeros((8, 128), F32) for _ in range(GROUPS + 1)]
    e = [jnp.zeros((8, 128), F32) for _ in range(GROUPS + 1)]
    for x in range(ROWS):
        for copy in copies[x]:
            copy.wait()
        for g in range(GROUPS + 1):
            first, last = uall[x, group(g), tile(0)], uall[x, group(g), tile(TILES - 1)]
            w[g] = jnp.where(lane == x, pltpu.roll(first, x, 1), w[g])
            e[g] = jnp.where(lane == x, pltpu.roll(last, x + 1, 1), e[g])
            if g < GROUPS:
                w[g] = jnp.where(lane == ROWS + x, pltpu.roll(first, ROWS + x - 1, 1), w[g])
                e[g] = jnp.where(lane == ROWS + x, pltpu.roll(last, ROWS + x + 2, 1), e[g])
    for g in range(GROUPS + 1):
        west[group(g), :] = w[g]
        east[group(g), :] = e[g]
        odd = odd_column_device()
        first_to[group(g), :] = jnp.where(odd, w[g], e[g])
        second_to[group(g), :] = jnp.where(odd, e[g], w[g])


def columns(initial, kappa, decay):
    col = pltpu.VMEM((EXT, 128), F32)
    return pl.pallas_call(
        column_kernel,
        name="columns",
        in_specs=[HBM] * 3,
        out_specs=[VM] * 5,
        out_shape=[pltpu.VMEM((ROWS, EXT, COLS), F32), col, col, col, col],
        scratch_shapes=[pltpu.SemaphoreType.DMA((3, ROWS))],
        compiler_params=params(54),
    )(initial, kappa, decay)


def corner_kernel(first_from, second_from, halo_w, halo_e, first_to, second_to):
    lane = lanes()
    odd, odd_row = odd_column_device(), odd_row_device()
    for g in range(GROUPS + 1):
        a, b = first_from[group(g), :], second_from[group(g), :]
        w, e = jnp.where(odd, a, b), jnp.where(odd, b, a)
        halo_w[group(g), :] = w
        halo_e[group(g), :] = e
        if g < GROUPS:
            top = jnp.where(lane == 0, w, pltpu.roll(e, 1, 1))
            w, e = pltpu.roll(w, 128 - (ROWS - 1), 1), pltpu.roll(e, 128 - (ROWS - 2), 1)
            bottom = jnp.where(lane == 0, w, e)
            first_to[group(g), :] = jnp.where(odd_row, top, bottom)
            second_to[group(g), :] = jnp.where(odd_row, bottom, top)


def corners(first_from, second_from):
    halo, message = pltpu.VMEM((EXT, 128), F32), pltpu.VMEM((S, 128), F32)
    return pl.pallas_call(
        corner_kernel,
        name="corners",
        in_specs=[VM] * 2,
        out_specs=[VM] * 4,
        out_shape=[halo, halo, message, message],
        compiler_params=params(2),
    )(first_from, second_from)


def fields(k):
    b = k * 0.2
    keep = 1.0 - jnp.broadcast_to(k[FIELDS : FIELDS + 1, :], (8, 128))
    return keep - 4.0 * b, b


def choose(k, f):
    return jnp.take_along_axis(k, f, axis=0, mode="promise_in_bounds")


def step_row(fi, load_field, center, above, below, edge_w, edge_e, emit):
    lane = lanes()
    low, high = lane == 0, lane == 127
    from_w = [edge_w(g) for g in range(GROUPS)]
    from_e = [pltpu.roll(center(g, 0), 127, 1) for g in range(GROUPS)]
    for t in range(TILES):
        ka, kb = fields(load_field(t))
        held = None
        for g in range(GROUPS):
            here = center(g, t)
            right = pltpu.roll(here, 1, 1)
            west = jnp.where(low, from_w[g], right)
            from_w[g] = right
            nxt = pltpu.roll(center(g, t + 1), 127, 1) if t + 1 < TILES else edge_e(g)
            east = jnp.where(high, nxt, from_e[g])
            from_e[g] = nxt
            a, b = choose(ka, fi[group(g), :]), choose(kb, fi[group(g), :])
            new = a * here + b * ((above(g, t) + below(g, t)) + (west + east))
            if g % 2 == 0:
                held = new
            else:
                emit(g - 1, t, held, new)


def split_store(ref, index, g, t, first, second):
    both = jnp.concatenate([first, second], 0)
    top = both.astype(BF16)
    ref[index, 8 * g : 8 * g + 16, tile(t)] = top
    ref[index, S + 8 * g : S + 8 * g + 16, tile(t)] = (both - top.astype(F32)).astype(BF16)


def gram(acc, f, s):
    hi = jnp.concatenate([f[:S, :], s[:S, :]], 0)
    rhs = jnp.concatenate([hi, f[S:, :], s[S:, :]], 0)
    acc[...] += lax.dot_general(hi, rhs, (((1,), (1,)), ((), ())), preferred_element_type=F32)


def column_step(fi, halo, own, g, up=None, down=None):
    lane = lanes()
    one = halo[group(g), :]
    two = pltpu.roll(one, 128 - ROWS, 1)
    ka, kb = fields(halo[S:EXT, :])
    a, b = choose(ka, fi[group(g), :]), choose(kb, fi[group(g), :])
    above, below = pltpu.roll(one, 1, 1), pltpu.roll(one, 127, 1)
    if up is not None:
        above = jnp.where(lane == 0, up, above)
        below = jnp.where(lane == ROWS - 1, down, below)
    return a * one + b * ((above + below) + (two + own[group(g), :]))


def interior_kernel(fi, uall, own_w, own_e, halo_w, halo_e, first, f0, f1, f2, s0, s1, s2, acc, col_w, col_e):
    acc[...] = jnp.zeros_like(acc)
    for g in range(GROUPS):
        col_w[group(g), :] = column_step(fi, halo_w, own_w, g)
        col_e[group(g), :] = column_step(fi, halo_e, own_e, g)

    def field(x):
        return lambda t: uall[x, S:EXT, tile(t)]

    def one(x, ref=None, index=None):
        def emit(g, t, p, q):
            first[x, group(g), tile(t)] = p
            first[x, group(g + 1), tile(t)] = q
            if ref is not None:
                split_store(ref, index, g, t, p, q)

        step_row(
            fi,
            field(x),
            lambda g, t: uall[x, group(g), tile(t)],
            lambda g, t: uall[x - 1, group(g), tile(t)],
            lambda g, t: uall[x + 1, group(g), tile(t)],
            lambda g: pltpu.roll(halo_w[group(g), :], (128 - x) % 128, 1),
            lambda g: pltpu.roll(halo_e[group(g), :], 127 - x, 1),
            emit,
        )

    def two(x, ref, index):
        step_row(
            fi,
            field(x),
            lambda g, t: first[x, group(g), tile(t)],
            lambda g, t: first[x - 1, group(g), tile(t)],
            lambda g, t: first[x + 1, group(g), tile(t)],
            lambda g: pltpu.roll(col_w[group(g), :], (128 - x) % 128, 1),
            lambda g: pltpu.roll(col_e[group(g), :], 127 - x, 1),
            lambda g, t, p, q: split_store(ref, index, g, t, p, q),
        )

    one(1)
    one(2, f0, 0)
    one(3, f1, 0)
    two(2, s0, 0)

    def body(i, carry):
        x = 4 + 3 * i
        gram(acc, f0[i], s0[i])
        one(x, f2, i)
        two(x - 1, s1, i)
        gram(acc, f1[i], s1[i])
        one(x + 1, f0, i + 1)
        two(x, s2, i)
        gram(acc, f2[i], s2[i])
        one(x + 2, f1, i + 1)
        two(x + 1, s0, i + 1)
        return carry

    lax.fori_loop(0, THIRD - 1, body, 0)
    end = THIRD - 1
    gram(acc, f0[end], s0[end])
    one(ROWS - 3, f2, end)
    two(ROWS - 4, s1, end)
    gram(acc, f1[end], s1[end])
    one(ROWS - 2)
    two(ROWS - 3, s2, end)
    gram(acc, f2[end], s2[end])


def interior(fi, uall, own_w, own_e, halo_w, halo_e):
    snap = pltpu.VMEM((THIRD, SNAP, COLS), BF16)
    return pl.pallas_call(
        interior_kernel,
        name="interior",
        in_specs=[VM] * 6,
        out_specs=[VM] * 8,
        out_shape=[pltpu.VMEM((ROWS, S, COLS), F32), *[snap] * 6, pltpu.VMEM((SNAP, 2 * SNAP), F32)],
        scratch_shapes=[pltpu.VMEM((S, 128), F32)] * 2,
        cost_estimate=pl.CostEstimate(flops=2 * 12 * SNAP * 2 * SNAP * COLS, bytes_accessed=2**25, transcendentals=0),
        compiler_params=params(8),
    )(fi, uall, own_w, own_e, halo_w, halo_e)


def edge_kernel(
    fi, uall, own_w, own_e, halo_w, halo_e, first, inner, n1, s1, nc, sc, snap_f, snap_s, keep, give, col_w, col_e, edge, acc, packed
):
    acc[...] = inner[...]
    odd = odd_row_device()
    for g in range(GROUPS):
        a, b = nc[group(g), :], sc[group(g), :]
        up, down = jnp.where(odd, a, b), jnp.where(odd, b, a)
        col_w[group(g), :] = column_step(fi, halo_w, own_w, g, up, pltpu.roll(down, ROWS - 1, 1))
        col_e[group(g), :] = column_step(fi, halo_e, own_e, g, pltpu.roll(up, 127, 1), pltpu.roll(down, ROWS - 2, 1))

    def rows(ref, base):
        return lambda g, t: ref[group(g), base + 128 * t : base + 128 * t + 128]

    def at(ref, x):
        return lambda g, t: ref[x, group(g), tile(t)]

    def field(x):
        return lambda t: uall[x, S:EXT, tile(t)]

    def pick(ref, x, to):
        return lambda g: pltpu.roll(ref[group(g), :], (to + 128 - x) & 127, 1)

    for near, corner, at_top in ((n1, nc, odd), (s1, sc, jnp.logical_not(odd))):
        row, inside, deeper = (jnp.where(at_top, i, ROWS - 1 - i) for i in range(3))

        def put(index):
            def emit(g, t, p, q):
                edge[index, group(g), tile(t)] = p
                edge[index, group(g + 1), tile(t)] = q

            return emit

        def put_both(index, target):
            def emit(g, t, p, q):
                put(index)(g, t, p, q)
                split_store(snap_f, target, g, t, p, q)

            return emit

        def put_second(target):
            return lambda g, t, p, q: split_store(snap_s, target, g, t, p, q)

        outer, inner_slot = jnp.where(at_top, 0, 3), jnp.where(at_top, 1, 2)
        step_row(
            fi,
            lambda t, near=near: near[8 * t : 8 * t + 8, FIELD : FIELD + 128],
            rows(near, 0),
            rows(near, COLS),
            at(uall, row),
            pick(corner, 0, 0),
            pick(corner, 1, 127),
            put(0),
        )
        step_row(
            fi, field(row), at(uall, row), rows(near, 0), at(uall, inside),
            pick(halo_w, row, 0), pick(halo_e, row, 127), put_both(1, outer),
        )
        step_row(
            fi, field(row), at(edge, 1), at(edge, 0), at(first, inside),
            pick(col_w, row, 0), pick(col_e, row, 127), put_second(outer),
        )
        step_row(
            fi, field(inside), at(first, inside), at(edge, 1), at(first, deeper),
            pick(col_w, inside, 0), pick(col_e, inside, 127), put_second(inner_slot),
        )
        for t in range(TILES):
            for g in range(0, GROUPS, 2):
                split_store(
                    snap_f, inner_slot, g, t,
                    first[inside, group(g), tile(t)], first[inside, group(g + 1), tile(t)],
                )
        gram(acc, snap_f[outer], snap_s[outer])
        gram(acc, snap_f[inner_slot], snap_s[inner_slot])
    cross = acc[:, SNAP:]
    full = acc[:, :SNAP] + (cross + cross.T)
    top, bottom = full[:S, :], pltpu.roll(full[S:, :], S, 1)
    r = lax.broadcasted_iota(jnp.int32, (S, SNAP), 0)
    c = lax.broadcasted_iota(jnp.int32, (S, SNAP), 1)
    packed[0:S, :] = jnp.where((c < S) & (r > c), bottom, top)
    diag = jnp.sum(jnp.where(r == c, bottom, 0.0), axis=0, keepdims=True)
    packed[S : S + 8, :] = jnp.where(lax.broadcasted_iota(jnp.int32, (8, SNAP), 0) == 0, diag, 0.0)
    packed[S + 8 :, :] = jnp.zeros((8, SNAP), F32)
    second = lax.axis_index("core") == 1
    a, b = packed[:HALF, :], packed[HALF:, :]
    keep[...] = jnp.where(second, b, a)
    give[...] = jnp.where(second, a, b)


def edges(fi, uall, own_w, own_e, halo_w, halo_e, first, inner, n1, s1, nc, sc):
    snap, half = pltpu.VMEM((4, SNAP, COLS), BF16), pltpu.VMEM((HALF, SNAP), F32)
    return pl.pallas_call(
        edge_kernel,
        name="edges",
        in_specs=[VM] * 12,
        out_specs=[VM] * 4,
        out_shape=[snap, snap, half, half],
        scratch_shapes=[
            pltpu.VMEM((S, 128), F32),
            pltpu.VMEM((S, 128), F32),
            pltpu.VMEM((2, S, COLS), F32),
            pltpu.VMEM((SNAP, 2 * SNAP), F32),
            pltpu.VMEM((2 * HALF, SNAP), F32),
        ],
        compiler_params=params(8),
    )(fi, uall, own_w, own_e, halo_w, halo_e, first, inner, n1, s1, nc, sc)


def unpack(packed):
    top, diag = packed[0:S, :], packed[S : S + 1, :]
    r = lax.broadcasted_iota(jnp.int32, (S, SNAP), 0)
    c = lax.broadcasted_iota(jnp.int32, (S, SNAP), 1)
    upper = jnp.where(r <= c, top, 0.0)
    lower = pltpu.roll(jnp.where((r > c) & (c < S), top, 0.0), S, 1)
    on_diag = jnp.where(r == c - S, pltpu.roll(jnp.broadcast_to(diag, (8, SNAP)), S, 1)[0:1, :], 0.0)
    zero = jnp.zeros_like(lower)
    return jnp.concatenate([upper, on_diag], 0) + jnp.concatenate([zero, lower], 0).T


def factor(m, z):
    sub = lax.broadcasted_iota(jnp.int32, (8, 128), 0)
    for k in range(SNAP // BLOCK):
        lo = k * BLOCK
        panel = m[lo : lo + BLOCK, :]
        p = {}
        for i in range(BLOCK):
            for j in range(i, BLOCK):
                p[i, j] = jnp.broadcast_to(panel[i : i + 1, lo + j : lo + j + 1], (8, 128))
        rows = [[jnp.broadcast_to(panel[i : i + 1, tile(h)], (8, 128)) for h in range(2)] for i in range(BLOCK)]
        for j in range(BLOCK):
            r = lax.rsqrt(p[j, j])
            u = {i: p[j, i] * r for i in range(j + 1, BLOCK)}
            for i in range(j + 1, BLOCK):
                for l in range(i, BLOCK):
                    p[i, l] = p[i, l] - u[i] * u[l]
            rows[j] = [v * r for v in rows[j]]
            for i in range(j + 1, BLOCK):
                rows[i] = [v - u[i] * w for v, w in zip(rows[i], rows[j])]
        for part in range(BLOCK // 8):
            for h in range(2):
                v = rows[8 * part][h]
                for i in range(1, 8):
                    v = jnp.where(sub == i, rows[8 * part + i][h], v)
                z[lo + 8 * part : lo + 8 * part + 8, tile(h)] = v
        if lo + BLOCK < SNAP:
            done = z[lo : lo + BLOCK, :]
            update = lax.dot_general(
                done[:, :SNAP], done, (((0,), (0,)), ((), ())),
                precision=lax.Precision.HIGHEST, preferred_element_type=F32,
            )
            m[lo + BLOCK :, :] = m[lo + BLOCK :, :] - update[lo + BLOCK :, :]


def basis_kernel(scale, mine, other, *refs):
    (*snaps, out, tri, m, z, buf, sems) = refs
    r = lax.broadcasted_iota(jnp.int32, (SNAP, SNAP), 0)
    c = lax.broadcasted_iota(jnp.int32, (SNAP, SNAP), 1)
    second = lax.axis_index("core") == 1
    a, b = mine[...], other[...]
    m[:, :SNAP] = unpack(jnp.concatenate([jnp.where(second, b, a), jnp.where(second, a, b)], 0))
    m[:, SNAP:] = jnp.where(r == c, 1.0, 0.0)
    factor(m, z)
    tri[...] = jnp.where(r <= c, z[:, :SNAP], 0.0) * (1.0 / scale)
    w = jnp.where(r >= c, z[:, SNAP:], 0.0) * scale
    top = w.astype(BF16)
    rest = (w - top.astype(F32)).astype(BF16)
    twice = jnp.concatenate([top, top], 1)

    def copy(x):
        return pltpu.make_async_copy(buf.at[x], out.at[:, x, :], sems.at[x])

    def row(x, f, s):
        hi = jnp.concatenate([f[:S, :], s[:S, :]], 0)
        both = jnp.concatenate([hi, f[S:, :], s[S:, :]], 0)
        buf[x] = jnp.dot(twice, both, preferred_element_type=F32) + jnp.dot(rest, hi, preferred_element_type=F32)
        copy(x).start()

    def body(i, carry):
        for k in range(3):
            row(2 + 3 * i + k, snaps[k][i], snaps[3 + k][i])
        return carry

    lax.fori_loop(0, THIRD, body, 0)
    for i, x in enumerate((0, 1, ROWS - 2, ROWS - 1)):
        row(x, snaps[6][i], snaps[7][i])
    for x in range(ROWS):
        copy(x).wait()


def make_basis(scale, mine, other, *snaps):
    def kernel(*refs):
        basis_kernel(scale, *refs)

    return pl.pallas_call(
        kernel,
        name="basis",
        in_specs=[VM] * 10,
        out_specs=[HBM, VM],
        out_shape=[
            jax.ShapeDtypeStruct((SNAP, ROWS, COLS), F32),
            jax.ShapeDtypeStruct((SNAP, SNAP), F32),
        ],
        scratch_shapes=[
            pltpu.VMEM((SNAP, 2 * SNAP), F32),
            pltpu.VMEM((SNAP, 2 * SNAP), F32),
            pltpu.VMEM((ROWS, SNAP, COLS), F32),
            pltpu.SemaphoreType.DMA((ROWS,)),
        ],
        compiler_params=params(16),
    )(mine, other, *snaps)


def spread_sum(value, axis):
    count = lax.axis_size(axis)
    every = lax.all_to_all(jnp.broadcast_to(value[None], (count, *value.shape)), axis, 0, 0)
    parts = [every[i] for i in range(count)]
    while len(parts) > 1:
        parts = [a + b for a, b in zip(parts[::2], parts[1::2], strict=True)]
    return parts[0]


def pairs(axis, start):
    lower = range(start, lax.axis_size(axis) - 1, 2)
    return [(i, i + 1) for i in lower] + [(i + 1, i) for i in lower]


def shards(initial, kappa, decay, field_index):
    fi = jnp.broadcast_to(field_index[:, None], (S, 128))
    row_a, row_b = rows(initial, kappa, decay)
    near_a, near_b = lax.ppermute(row_a, ROWAXIS, pairs(ROWAXIS, 0)), lax.ppermute(row_b, ROWAXIS, pairs(ROWAXIS, 1))
    uall, own_w, own_e, col_a, col_b = columns(initial, kappa, decay)
    col_a, col_b = lax.ppermute(col_a, COLAXIS, pairs(COLAXIS, 0)), lax.ppermute(col_b, COLAXIS, pairs(COLAXIS, 1))
    halo_w, halo_e, corner_a, corner_b = corners(col_a, col_b)
    corner_a = lax.ppermute(corner_a, ROWAXIS, pairs(ROWAXIS, 0))
    corner_b = lax.ppermute(corner_b, ROWAXIS, pairs(ROWAXIS, 1))
    first, *inner_snaps, inner = interior(fi, uall, own_w, own_e, halo_w, halo_e)
    edge_f, edge_s, keep, give = edges(
        fi, uall, own_w, own_e, halo_w, halo_e, first, inner, near_a, near_b, corner_a, corner_b
    )
    swap = [(0, 1), (1, 0)]
    mine = keep + lax.ppermute(give, "core", swap)
    mine = spread_sum(spread_sum(mine, ("x", "y")), "z")
    other = lax.ppermute(mine, "core", swap)
    cells = lax.axis_size(ROWAXIS) * lax.axis_size(COLAXIS) * ROWS * COLS
    return make_basis(math.sqrt(cells), mine, other, *inner_snaps, edge_f, edge_s)


def solution(mesh):
    wide, narrow = mesh.devices.shape
    fine = Mesh(mesh.devices.reshape(wide // 4, 4, narrow // 2, 2), ("z", "x", "y", "core"))
    grid = P(None, ROWAXIS, COLAXIS)
    return jax.shard_map(
        shards,
        mesh=fine,
        in_specs=(grid, grid, P(ROWAXIS, COLAXIS), P()),
        out_specs=(grid, P()),
        check_vma=False,
    )
```

```python
import math

import jax
import jax.numpy as jnp
from jax import lax
from jax.experimental import pallas as pl
from jax.experimental.pallas import tpu as pltpu
from jax.sharding import Mesh, PartitionSpec as P

F32, BF16 = jnp.float32, jnp.bfloat16
S, ROWS, COLS, FIELDS = 64, 16, 1024, 4
SNAP = 2 * S
TILES, GROUPS = COLS // 128, S // 8
EXT = S + 8
KAP, DEC = S, S + FIELDS
HALF = (S + 16) // 2
THIRD = (ROWS - 4) // 3
BLOCK = 16
ROWAXIS, COLAXIS = ("z", "x"), ("y", "core")
FIELD, MESSAGE = 2 * COLS, 2 * COLS + 128
HBM = pl.BlockSpec(memory_space=pltpu.HBM)
VM = pl.BlockSpec(memory_space=pltpu.VMEM)


def params(mib):
    return pltpu.CompilerParams(vmem_limit_bytes=mib * 2**20)


def lanes():
    return lax.broadcasted_iota(jnp.int32, (8, 128), 1)


def tile(t):
    return slice(128 * t, 128 * t + 128)


def group(g):
    return slice(8 * g, 8 * g + 8)


def odd_row_device():
    return (lax.axis_index("x") & 1) == 1


def odd_column_device():
    return lax.axis_index("core") == 1


def message_kernel(u, kap, dec, index, uall, west, east, row_a, row_b, col_a, col_b, fi, sems, scalars, index_sem):
    index_copy = pltpu.make_async_copy(index, scalars, index_sem)
    index_copy.start()
    for x in range(ROWS):
        uall[x, S:EXT, :] = jnp.zeros((8, COLS), F32)
    copies = []
    for x in range(ROWS):
        copies.append(
            (
                pltpu.make_async_copy(u.at[:, x, :], uall.at[x, 0:S, :], sems.at[0, x]),
                pltpu.make_async_copy(kap.at[:, x, :], uall.at[x, KAP : KAP + FIELDS, :], sems.at[1, x]),
                pltpu.make_async_copy(dec.at[x : x + 1, :], uall.at[x, DEC : DEC + 1, :], sems.at[2, x]),
            )
        )
        for copy in copies[x]:
            copy.start()
    index_copy.wait()
    sub = lax.broadcasted_iota(jnp.int32, (8, 128), 0)
    for g in range(GROUPS):
        v = jnp.full((8, 128), scalars[8 * g], jnp.int32)
        for i in range(1, 8):
            v = jnp.where(sub == i, scalars[8 * g + i], v)
        fi[group(g), :] = v
    lane = lanes()
    w = [jnp.zeros((8, 128), F32) for _ in range(GROUPS + 1)]
    e = [jnp.zeros((8, 128), F32) for _ in range(GROUPS + 1)]
    for x in range(ROWS):
        for copy in copies[x]:
            copy.wait()
        for g in range(GROUPS + 1):
            first, last = uall[x, group(g), tile(0)], uall[x, group(g), tile(TILES - 1)]
            w[g] = jnp.where(lane == x, pltpu.roll(first, x, 1), w[g])
            e[g] = jnp.where(lane == x, pltpu.roll(last, x + 1, 1), e[g])
            if g < GROUPS:
                w[g] = jnp.where(lane == ROWS + x, pltpu.roll(first, ROWS + x - 1, 1), w[g])
                e[g] = jnp.where(lane == ROWS + x, pltpu.roll(last, ROWS + x + 2, 1), e[g])
    odd = odd_column_device()
    for g in range(GROUPS + 1):
        west[group(g), :] = w[g]
        east[group(g), :] = e[g]
        col_a[group(g), :] = jnp.where(odd, w[g], e[g])
        col_b[group(g), :] = jnp.where(odd, e[g], w[g])
    odd = odd_row_device()
    for to, top in ((row_a, odd), (row_b, jnp.logical_not(odd))):
        near, far = jnp.where(top, 0, ROWS - 1), jnp.where(top, 1, ROWS - 2)
        to[:, 0:COLS] = uall[near, 0:S, :]
        to[:, COLS : 2 * COLS] = uall[far, 0:S, :]
        for t in range(TILES):
            to[8 * t : 8 * t + 8, FIELD : FIELD + 128] = uall[near, S:EXT, tile(t)]


def messages(initial, kappa, decay, field_index):
    row, col = pltpu.VMEM((S, MESSAGE), F32), pltpu.VMEM((EXT, 128), F32)
    return pl.pallas_call(
        message_kernel,
        name="messages",
        in_specs=[HBM] * 4,
        out_specs=[VM] * 8,
        out_shape=[
            pltpu.VMEM((ROWS, EXT, COLS), F32), col, col, row, row, col, col, pltpu.VMEM((S, 128), jnp.int32),
        ],
        scratch_shapes=[
            pltpu.SemaphoreType.DMA((3, ROWS)), pltpu.SMEM((S,), jnp.int32), pltpu.SemaphoreType.DMA(()),
        ],
        compiler_params=params(52),
    )(initial, kappa, decay, field_index)


def corner_kernel(first_from, second_from, halo_w, halo_e, first_to, second_to):
    lane = lanes()
    odd, odd_row = odd_column_device(), odd_row_device()
    for g in range(GROUPS + 1):
        a, b = first_from[group(g), :], second_from[group(g), :]
        w, e = jnp.where(odd, a, b), jnp.where(odd, b, a)
        halo_w[group(g), :] = w
        halo_e[group(g), :] = e
        if g < GROUPS:
            top = jnp.where(lane == 0, w, pltpu.roll(e, 1, 1))
            w, e = pltpu.roll(w, 128 - (ROWS - 1), 1), pltpu.roll(e, 128 - (ROWS - 2), 1)
            bottom = jnp.where(lane == 0, w, e)
            first_to[group(g), :] = jnp.where(odd_row, top, bottom)
            second_to[group(g), :] = jnp.where(odd_row, bottom, top)


def corners(first_from, second_from):
    halo, message = pltpu.VMEM((EXT, 128), F32), pltpu.VMEM((S, 128), F32)
    return pl.pallas_call(
        corner_kernel,
        name="corners",
        in_specs=[VM] * 2,
        out_specs=[VM] * 4,
        out_shape=[halo, halo, message, message],
        compiler_params=params(2),
    )(first_from, second_from)


def fields(k):
    b = k * 0.2
    keep = 1.0 - jnp.broadcast_to(k[FIELDS : FIELDS + 1, :], (8, 128))
    return keep - 4.0 * b, b


def choose(k, f):
    return jnp.take_along_axis(k, f, axis=0, mode="promise_in_bounds")


def step_row(fi, load_field, center, above, below, edge_w, edge_e, emit):
    lane = lanes()
    low, high = lane == 0, lane == 127
    from_w = [edge_w(g) for g in range(GROUPS)]
    from_e = [pltpu.roll(center(g, 0), 127, 1) for g in range(GROUPS)]
    for t in range(TILES):
        ka, kb = fields(load_field(t))
        held = None
        for g in range(GROUPS):
            here = center(g, t)
            right = pltpu.roll(here, 1, 1)
            west = jnp.where(low, from_w[g], right)
            from_w[g] = right
            nxt = pltpu.roll(center(g, t + 1), 127, 1) if t + 1 < TILES else edge_e(g)
            east = jnp.where(high, nxt, from_e[g])
            from_e[g] = nxt
            a, b = choose(ka, fi[group(g), :]), choose(kb, fi[group(g), :])
            new = a * here + b * ((above(g, t) + below(g, t)) + (west + east))
            if g % 2 == 0:
                held = new
            else:
                emit(g - 1, t, held, new)


def split_store(ref, index, g, t, first, second):
    both = jnp.concatenate([first, second], 0)
    top = both.astype(BF16)
    ref[index, 8 * g : 8 * g + 16, tile(t)] = top
    ref[index, S + 8 * g : S + 8 * g + 16, tile(t)] = (both - top.astype(F32)).astype(BF16)


def gram(acc, f, s):
    hi = jnp.concatenate([f[:S, :], s[:S, :]], 0)
    rhs = jnp.concatenate([hi, f[S:, :], s[S:, :]], 0)
    acc[...] += lax.dot_general(hi, rhs, (((1,), (1,)), ((), ())), preferred_element_type=F32)


def column_step(fi, halo, own, g, up=None, down=None):
    lane = lanes()
    one = halo[group(g), :]
    two = pltpu.roll(one, 128 - ROWS, 1)
    ka, kb = fields(halo[S:EXT, :])
    a, b = choose(ka, fi[group(g), :]), choose(kb, fi[group(g), :])
    above, below = pltpu.roll(one, 1, 1), pltpu.roll(one, 127, 1)
    if up is not None:
        above = jnp.where(lane == 0, up, above)
        below = jnp.where(lane == ROWS - 1, down, below)
    return a * one + b * ((above + below) + (two + own[group(g), :]))


def interior_kernel(fi, uall, own_w, own_e, halo_w, halo_e, first, f0, f1, f2, s0, s1, s2, acc, col_w, col_e):
    acc[...] = jnp.zeros_like(acc)
    for g in range(GROUPS):
        col_w[group(g), :] = column_step(fi, halo_w, own_w, g)
        col_e[group(g), :] = column_step(fi, halo_e, own_e, g)

    def field(x):
        return lambda t: uall[x, S:EXT, tile(t)]

    def one(x, ref=None, index=None):
        def emit(g, t, p, q):
            first[x, group(g), tile(t)] = p
            first[x, group(g + 1), tile(t)] = q
            if ref is not None:
                split_store(ref, index, g, t, p, q)

        step_row(
            fi,
            field(x),
            lambda g, t: uall[x, group(g), tile(t)],
            lambda g, t: uall[x - 1, group(g), tile(t)],
            lambda g, t: uall[x + 1, group(g), tile(t)],
            lambda g: pltpu.roll(halo_w[group(g), :], (128 - x) % 128, 1),
            lambda g: pltpu.roll(halo_e[group(g), :], 127 - x, 1),
            emit,
        )

    def two(x, ref, index):
        step_row(
            fi,
            field(x),
            lambda g, t: first[x, group(g), tile(t)],
            lambda g, t: first[x - 1, group(g), tile(t)],
            lambda g, t: first[x + 1, group(g), tile(t)],
            lambda g: pltpu.roll(col_w[group(g), :], (128 - x) % 128, 1),
            lambda g: pltpu.roll(col_e[group(g), :], 127 - x, 1),
            lambda g, t, p, q: split_store(ref, index, g, t, p, q),
        )

    one(1)
    one(2, f0, 0)
    one(3, f1, 0)
    two(2, s0, 0)

    def body(i, carry):
        x = 4 + 3 * i
        gram(acc, f0[i], s0[i])
        one(x, f2, i)
        two(x - 1, s1, i)
        gram(acc, f1[i], s1[i])
        one(x + 1, f0, i + 1)
        two(x, s2, i)
        gram(acc, f2[i], s2[i])
        one(x + 2, f1, i + 1)
        two(x + 1, s0, i + 1)
        return carry

    lax.fori_loop(0, THIRD - 1, body, 0)
    end = THIRD - 1
    gram(acc, f0[end], s0[end])
    one(ROWS - 3, f2, end)
    two(ROWS - 4, s1, end)
    gram(acc, f1[end], s1[end])
    one(ROWS - 2)
    two(ROWS - 3, s2, end)
    gram(acc, f2[end], s2[end])


def interior(fi, uall, own_w, own_e, halo_w, halo_e):
    snap = pltpu.VMEM((THIRD, SNAP, COLS), BF16)
    return pl.pallas_call(
        interior_kernel,
        name="interior",
        in_specs=[VM] * 6,
        out_specs=[VM] * 8,
        out_shape=[pltpu.VMEM((ROWS, S, COLS), F32), *[snap] * 6, pltpu.VMEM((SNAP, 2 * SNAP), F32)],
        scratch_shapes=[pltpu.VMEM((S, 128), F32)] * 2,
        cost_estimate=pl.CostEstimate(flops=2 * 12 * SNAP * 2 * SNAP * COLS, bytes_accessed=2**25, transcendentals=0),
        compiler_params=params(8),
    )(fi, uall, own_w, own_e, halo_w, halo_e)


def edge_kernel(
    fi, uall, own_w, own_e, halo_w, halo_e, first, inner, n1, s1, nc, sc, snap_f, snap_s, keep, give, col_w, col_e, edge, acc, packed
):
    acc[...] = inner[...]
    odd = odd_row_device()
    for g in range(GROUPS):
        a, b = nc[group(g), :], sc[group(g), :]
        up, down = jnp.where(odd, a, b), jnp.where(odd, b, a)
        col_w[group(g), :] = column_step(fi, halo_w, own_w, g, up, pltpu.roll(down, ROWS - 1, 1))
        col_e[group(g), :] = column_step(fi, halo_e, own_e, g, pltpu.roll(up, 127, 1), pltpu.roll(down, ROWS - 2, 1))

    def rows(ref, base):
        return lambda g, t: ref[group(g), base + 128 * t : base + 128 * t + 128]

    def at(ref, x):
        return lambda g, t: ref[x, group(g), tile(t)]

    def field(x):
        return lambda t: uall[x, S:EXT, tile(t)]

    def pick(ref, x, to):
        return lambda g: pltpu.roll(ref[group(g), :], (to + 128 - x) & 127, 1)

    for near, corner, at_top in ((n1, nc, odd), (s1, sc, jnp.logical_not(odd))):
        row, inside, deeper = (jnp.where(at_top, i, ROWS - 1 - i) for i in range(3))

        def put(index):
            def emit(g, t, p, q):
                edge[index, group(g), tile(t)] = p
                edge[index, group(g + 1), tile(t)] = q

            return emit

        def put_both(index, target):
            def emit(g, t, p, q):
                put(index)(g, t, p, q)
                split_store(snap_f, target, g, t, p, q)

            return emit

        def put_second(target):
            return lambda g, t, p, q: split_store(snap_s, target, g, t, p, q)

        outer, inner_slot = jnp.where(at_top, 0, 3), jnp.where(at_top, 1, 2)
        step_row(
            fi,
            lambda t, near=near: near[8 * t : 8 * t + 8, FIELD : FIELD + 128],
            rows(near, 0),
            rows(near, COLS),
            at(uall, row),
            pick(corner, 0, 0),
            pick(corner, 1, 127),
            put(0),
        )
        step_row(
            fi, field(row), at(uall, row), rows(near, 0), at(uall, inside),
            pick(halo_w, row, 0), pick(halo_e, row, 127), put_both(1, outer),
        )
        step_row(
            fi, field(row), at(edge, 1), at(edge, 0), at(first, inside),
            pick(col_w, row, 0), pick(col_e, row, 127), put_second(outer),
        )
        step_row(
            fi, field(inside), at(first, inside), at(edge, 1), at(first, deeper),
            pick(col_w, inside, 0), pick(col_e, inside, 127), put_second(inner_slot),
        )
        for t in range(TILES):
            for g in range(0, GROUPS, 2):
                split_store(
                    snap_f, inner_slot, g, t,
                    first[inside, group(g), tile(t)], first[inside, group(g + 1), tile(t)],
                )
        gram(acc, snap_f[outer], snap_s[outer])
        gram(acc, snap_f[inner_slot], snap_s[inner_slot])
    cross = acc[:, SNAP:]
    full = acc[:, :SNAP] + (cross + cross.T)
    top, bottom = full[:S, :], pltpu.roll(full[S:, :], S, 1)
    r = lax.broadcasted_iota(jnp.int32, (S, SNAP), 0)
    c = lax.broadcasted_iota(jnp.int32, (S, SNAP), 1)
    packed[0:S, :] = jnp.where((c < S) & (r > c), bottom, top)
    diag = jnp.sum(jnp.where(r == c, bottom, 0.0), axis=0, keepdims=True)
    packed[S : S + 8, :] = jnp.where(lax.broadcasted_iota(jnp.int32, (8, SNAP), 0) == 0, diag, 0.0)
    packed[S + 8 :, :] = jnp.zeros((8, SNAP), F32)
    second = lax.axis_index("core") == 1
    a, b = packed[:HALF, :], packed[HALF:, :]
    keep[...] = jnp.where(second, b, a)
    give[...] = jnp.where(second, a, b)


def edges(fi, uall, own_w, own_e, halo_w, halo_e, first, inner, n1, s1, nc, sc):
    snap, half = pltpu.VMEM((4, SNAP, COLS), BF16), pltpu.VMEM((HALF, SNAP), F32)
    return pl.pallas_call(
        edge_kernel,
        name="edges",
        in_specs=[VM] * 12,
        out_specs=[VM] * 4,
        out_shape=[snap, snap, half, half],
        scratch_shapes=[
            pltpu.VMEM((S, 128), F32),
            pltpu.VMEM((S, 128), F32),
            pltpu.VMEM((2, S, COLS), F32),
            pltpu.VMEM((SNAP, 2 * SNAP), F32),
            pltpu.VMEM((2 * HALF, SNAP), F32),
        ],
        compiler_params=params(8),
    )(fi, uall, own_w, own_e, halo_w, halo_e, first, inner, n1, s1, nc, sc)


def unpack(packed):
    top, diag = packed[0:S, :], packed[S : S + 1, :]
    r = lax.broadcasted_iota(jnp.int32, (S, SNAP), 0)
    c = lax.broadcasted_iota(jnp.int32, (S, SNAP), 1)
    upper = jnp.where(r <= c, top, 0.0)
    lower = pltpu.roll(jnp.where((r > c) & (c < S), top, 0.0), S, 1)
    on_diag = jnp.where(r == c - S, pltpu.roll(jnp.broadcast_to(diag, (8, SNAP)), S, 1)[0:1, :], 0.0)
    zero = jnp.zeros_like(lower)
    return jnp.concatenate([upper, on_diag], 0) + jnp.concatenate([zero, lower], 0).T


def factor(m, z):
    sub = lax.broadcasted_iota(jnp.int32, (8, 128), 0)
    for k in range(SNAP // BLOCK):
        lo = k * BLOCK
        panel = m[lo : lo + BLOCK, :]
        p = {}
        for i in range(BLOCK):
            for j in range(i, BLOCK):
                p[i, j] = jnp.broadcast_to(panel[i : i + 1, lo + j : lo + j + 1], (8, 128))
        rows = [[jnp.broadcast_to(panel[i : i + 1, tile(h)], (8, 128)) for h in range(2)] for i in range(BLOCK)]
        for j in range(BLOCK):
            r = lax.rsqrt(p[j, j])
            u = {i: p[j, i] * r for i in range(j + 1, BLOCK)}
            for i in range(j + 1, BLOCK):
                for l in range(i, BLOCK):
                    p[i, l] = p[i, l] - u[i] * u[l]
            rows[j] = [v * r for v in rows[j]]
            for i in range(j + 1, BLOCK):
                rows[i] = [v - u[i] * w for v, w in zip(rows[i], rows[j])]
        for part in range(BLOCK // 8):
            for h in range(2):
                v = rows[8 * part][h]
                for i in range(1, 8):
                    v = jnp.where(sub == i, rows[8 * part + i][h], v)
                z[lo + 8 * part : lo + 8 * part + 8, tile(h)] = v
        if lo + BLOCK < SNAP:
            done = z[lo : lo + BLOCK, :]
            high = done.astype(BF16)
            left_over = done - high.astype(F32)
            mid = left_over.astype(BF16)
            low = (left_over - mid.astype(F32)).astype(BF16)
            left = jnp.concatenate([high, high, mid, high, low, mid], 0)[:, :SNAP]
            right = jnp.concatenate([high, mid, high, low, high, mid], 0)
            update = lax.dot_general(left, right, (((0,), (0,)), ((), ())), preferred_element_type=F32)
            m[lo + BLOCK :, :] = m[lo + BLOCK :, :] - update[lo + BLOCK :, :]


def basis_kernel(scale, mine, other, *refs):
    (*snaps, out, tri, m, z, buf, sems) = refs
    r = lax.broadcasted_iota(jnp.int32, (SNAP, SNAP), 0)
    c = lax.broadcasted_iota(jnp.int32, (SNAP, SNAP), 1)
    second = lax.axis_index("core") == 1
    a, b = mine[...], other[...]
    m[:, :SNAP] = unpack(jnp.concatenate([jnp.where(second, b, a), jnp.where(second, a, b)], 0))
    m[:, SNAP:] = jnp.where(r == c, 1.0, 0.0)
    factor(m, z)
    tri[...] = jnp.where(r <= c, z[:, :SNAP], 0.0) * (1.0 / scale)
    w = jnp.where(r >= c, z[:, SNAP:], 0.0) * scale
    top = w.astype(BF16)
    rest = (w - top.astype(F32)).astype(BF16)
    twice = jnp.concatenate([top, top], 1)

    def copy(x):
        return pltpu.make_async_copy(buf.at[x], out.at[:, x, :], sems.at[x])

    def row(x, f, s):
        hi = jnp.concatenate([f[:S, :], s[:S, :]], 0)
        both = jnp.concatenate([hi, f[S:, :], s[S:, :]], 0)
        buf[x] = jnp.dot(twice, both, preferred_element_type=F32) + jnp.dot(rest, hi, preferred_element_type=F32)
        copy(x).start()

    def body(i, carry):
        for k in range(3):
            row(2 + 3 * i + k, snaps[k][i], snaps[3 + k][i])
        return carry

    lax.fori_loop(0, THIRD, body, 0)
    for i, x in enumerate((0, 1, ROWS - 2, ROWS - 1)):
        row(x, snaps[6][i], snaps[7][i])
    for x in range(ROWS):
        copy(x).wait()


def make_basis(scale, mine, other, *snaps):
    def kernel(*refs):
        basis_kernel(scale, *refs)

    return pl.pallas_call(
        kernel,
        name="basis",
        in_specs=[VM] * 10,
        out_specs=[HBM, VM],
        out_shape=[
            jax.ShapeDtypeStruct((SNAP, ROWS, COLS), F32),
            jax.ShapeDtypeStruct((SNAP, SNAP), F32),
        ],
        scratch_shapes=[
            pltpu.VMEM((SNAP, 2 * SNAP), F32),
            pltpu.VMEM((SNAP, 2 * SNAP), F32),
            pltpu.VMEM((ROWS, SNAP, COLS), F32),
            pltpu.SemaphoreType.DMA((ROWS,)),
        ],
        compiler_params=params(16),
    )(mine, other, *snaps)


def spread_sum(value, axis):
    count = lax.axis_size(axis)
    every = lax.all_to_all(jnp.broadcast_to(value[None], (count, *value.shape)), axis, 0, 0)
    parts = [every[i] for i in range(count)]
    while len(parts) > 1:
        parts = [a + b for a, b in zip(parts[::2], parts[1::2], strict=True)]
    return parts[0]


def pairs(axis, start):
    lower = range(start, lax.axis_size(axis) - 1, 2)
    return [(i, i + 1) for i in lower] + [(i + 1, i) for i in lower]


def shards(initial, kappa, decay, field_index):
    uall, own_w, own_e, row_a, row_b, col_a, col_b, fi = messages(initial, kappa, decay, field_index)
    near_a, near_b = lax.ppermute(row_a, ROWAXIS, pairs(ROWAXIS, 0)), lax.ppermute(row_b, ROWAXIS, pairs(ROWAXIS, 1))
    col_a, col_b = lax.ppermute(col_a, COLAXIS, pairs(COLAXIS, 0)), lax.ppermute(col_b, COLAXIS, pairs(COLAXIS, 1))
    halo_w, halo_e, corner_a, corner_b = corners(col_a, col_b)
    corner_a = lax.ppermute(corner_a, ROWAXIS, pairs(ROWAXIS, 0))
    corner_b = lax.ppermute(corner_b, ROWAXIS, pairs(ROWAXIS, 1))
    first, *inner_snaps, inner = interior(fi, uall, own_w, own_e, halo_w, halo_e)
    edge_f, edge_s, keep, give = edges(
        fi, uall, own_w, own_e, halo_w, halo_e, first, inner, near_a, near_b, corner_a, corner_b
    )
    swap = [(0, 1), (1, 0)]
    mine = keep + lax.ppermute(give, "core", swap)
    mine = spread_sum(spread_sum(mine, ("x", "y")), "z")
    other = lax.ppermute(mine, "core", swap)
    cells = lax.axis_size(ROWAXIS) * lax.axis_size(COLAXIS) * ROWS * COLS
    return make_basis(math.sqrt(cells), mine, other, *inner_snaps, edge_f, edge_s)


def solution(mesh):
    wide, narrow = mesh.devices.shape
    fine = Mesh(mesh.devices.reshape(wide // 4, 4, narrow // 2, 2), ("z", "x", "y", "core"))
    grid = P(None, ROWAXIS, COLAXIS)
    return jax.shard_map(
        shards,
        mesh=fine,
        in_specs=(grid, grid, P(ROWAXIS, COLAXIS), P()),
        out_specs=(grid, P()),
        check_vma=False,
    )
```

```python
import math

import jax
import jax.numpy as jnp
from jax import lax
from jax.experimental import pallas as pl
from jax.experimental.pallas import tpu as pltpu
from jax.sharding import Mesh, PartitionSpec as P

F32, BF16 = jnp.float32, jnp.bfloat16
S, ROWS, COLS, FIELDS = 64, 16, 1024, 4
SNAP = 2 * S
TILES, GROUPS = COLS // 128, S // 8
EXT = S + 8
KAP, DEC = S, S + FIELDS
HALF = (S + 16) // 2
THIRD = (ROWS - 4) // 3
BLOCK = 16
ROWAXIS, COLAXIS = ("z", "x"), ("y", "core")
FIELD, MESSAGE = 2 * COLS, 2 * COLS + 128
HBM = pl.BlockSpec(memory_space=pltpu.HBM)
VM = pl.BlockSpec(memory_space=pltpu.VMEM)


def params(mib):
    return pltpu.CompilerParams(vmem_limit_bytes=mib * 2**20)


def lanes():
    return lax.broadcasted_iota(jnp.int32, (8, 128), 1)


def tile(t):
    return slice(128 * t, 128 * t + 128)


def group(g):
    return slice(8 * g, 8 * g + 8)


def odd_row_device():
    return (lax.axis_index("x") & 1) == 1


def odd_column_device():
    return lax.axis_index("core") == 1


def message_kernel(u, kap, dec, index, uall, west, east, row_a, row_b, col_a, col_b, fi, sems, scalars, index_sem):
    index_copy = pltpu.make_async_copy(index, scalars, index_sem)
    index_copy.start()
    for x in range(ROWS):
        uall[x, S:EXT, :] = jnp.zeros((8, COLS), F32)
    copies = []
    for x in range(ROWS):
        copies.append(
            (
                pltpu.make_async_copy(u.at[:, x, :], uall.at[x, 0:S, :], sems.at[0, x]),
                pltpu.make_async_copy(kap.at[:, x, :], uall.at[x, KAP : KAP + FIELDS, :], sems.at[1, x]),
                pltpu.make_async_copy(dec.at[x : x + 1, :], uall.at[x, DEC : DEC + 1, :], sems.at[2, x]),
            )
        )
        for copy in copies[x]:
            copy.start()
    index_copy.wait()
    sub = lax.broadcasted_iota(jnp.int32, (8, 128), 0)
    for g in range(GROUPS):
        v = jnp.full((8, 128), scalars[8 * g], jnp.int32)
        for i in range(1, 8):
            v = jnp.where(sub == i, scalars[8 * g + i], v)
        fi[group(g), :] = v
    lane = lanes()
    w = [jnp.zeros((8, 128), F32) for _ in range(GROUPS + 1)]
    e = [jnp.zeros((8, 128), F32) for _ in range(GROUPS + 1)]
    for x in range(ROWS):
        for copy in copies[x]:
            copy.wait()
        for g in range(GROUPS + 1):
            first, last = uall[x, group(g), tile(0)], uall[x, group(g), tile(TILES - 1)]
            w[g] = jnp.where(lane == x, pltpu.roll(first, x, 1), w[g])
            e[g] = jnp.where(lane == x, pltpu.roll(last, x + 1, 1), e[g])
            if g < GROUPS:
                w[g] = jnp.where(lane == ROWS + x, pltpu.roll(first, ROWS + x - 1, 1), w[g])
                e[g] = jnp.where(lane == ROWS + x, pltpu.roll(last, ROWS + x + 2, 1), e[g])
    odd = odd_column_device()
    for g in range(GROUPS + 1):
        west[group(g), :] = w[g]
        east[group(g), :] = e[g]
        col_a[group(g), :] = jnp.where(odd, w[g], e[g])
        col_b[group(g), :] = jnp.where(odd, e[g], w[g])
    odd = odd_row_device()
    for to, top in ((row_a, odd), (row_b, jnp.logical_not(odd))):
        near, far = jnp.where(top, 0, ROWS - 1), jnp.where(top, 1, ROWS - 2)
        to[:, 0:COLS] = uall[near, 0:S, :]
        to[:, COLS : 2 * COLS] = uall[far, 0:S, :]
        for t in range(TILES):
            to[8 * t : 8 * t + 8, FIELD : FIELD + 128] = uall[near, S:EXT, tile(t)]


def messages(initial, kappa, decay, field_index):
    row, col = pltpu.VMEM((S, MESSAGE), F32), pltpu.VMEM((EXT, 128), F32)
    return pl.pallas_call(
        message_kernel,
        name="messages",
        in_specs=[HBM] * 4,
        out_specs=[VM] * 8,
        out_shape=[
            pltpu.VMEM((ROWS, EXT, COLS), F32), col, col, row, row, col, col, pltpu.VMEM((S, 128), jnp.int32),
        ],
        scratch_shapes=[
            pltpu.SemaphoreType.DMA((3, ROWS)), pltpu.SMEM((S,), jnp.int32), pltpu.SemaphoreType.DMA(()),
        ],
        compiler_params=params(52),
    )(initial, kappa, decay, field_index)


def corner_kernel(first_from, second_from, halo_w, halo_e, first_to, second_to):
    lane = lanes()
    odd, odd_row = odd_column_device(), odd_row_device()
    for g in range(GROUPS + 1):
        a, b = first_from[group(g), :], second_from[group(g), :]
        w, e = jnp.where(odd, a, b), jnp.where(odd, b, a)
        halo_w[group(g), :] = w
        halo_e[group(g), :] = e
        if g < GROUPS:
            top = jnp.where(lane == 0, w, pltpu.roll(e, 1, 1))
            w, e = pltpu.roll(w, 128 - (ROWS - 1), 1), pltpu.roll(e, 128 - (ROWS - 2), 1)
            bottom = jnp.where(lane == 0, w, e)
            first_to[group(g), :] = jnp.where(odd_row, top, bottom)
            second_to[group(g), :] = jnp.where(odd_row, bottom, top)


def corners(first_from, second_from):
    halo, message = pltpu.VMEM((EXT, 128), F32), pltpu.VMEM((S, 128), F32)
    return pl.pallas_call(
        corner_kernel,
        name="corners",
        in_specs=[VM] * 2,
        out_specs=[VM] * 4,
        out_shape=[halo, halo, message, message],
        compiler_params=params(2),
    )(first_from, second_from)


def fields(k):
    b = k * 0.2
    keep = 1.0 - jnp.broadcast_to(k[FIELDS : FIELDS + 1, :], (8, 128))
    return keep - 4.0 * b, b


def choose(k, f):
    return jnp.take_along_axis(k, f, axis=0, mode="promise_in_bounds")


def step_row(fi, load_field, center, above, below, edge_w, edge_e, emit):
    lane = lanes()
    low, high = lane == 0, lane == 127
    from_w = [edge_w(g) for g in range(GROUPS)]
    from_e = [pltpu.roll(center(g, 0), 127, 1) for g in range(GROUPS)]
    for t in range(TILES):
        ka, kb = fields(load_field(t))
        held = None
        for g in range(GROUPS):
            here = center(g, t)
            right = pltpu.roll(here, 1, 1)
            west = jnp.where(low, from_w[g], right)
            from_w[g] = right
            nxt = pltpu.roll(center(g, t + 1), 127, 1) if t + 1 < TILES else edge_e(g)
            east = jnp.where(high, nxt, from_e[g])
            from_e[g] = nxt
            a, b = choose(ka, fi[group(g), :]), choose(kb, fi[group(g), :])
            new = a * here + b * ((above(g, t) + below(g, t)) + (west + east))
            if g % 2 == 0:
                held = new
            else:
                emit(g - 1, t, held, new)


def split_store(ref, index, g, t, first, second):
    both = jnp.concatenate([first, second], 0)
    top = both.astype(BF16)
    ref[index, 8 * g : 8 * g + 16, tile(t)] = top
    ref[index, S + 8 * g : S + 8 * g + 16, tile(t)] = (both - top.astype(F32)).astype(BF16)


def gram(acc, f, s):
    hi = jnp.concatenate([f[:S, :], s[:S, :]], 0)
    rhs = jnp.concatenate([hi, f[S:, :], s[S:, :]], 0)
    acc[...] += lax.dot_general(hi, rhs, (((1,), (1,)), ((), ())), preferred_element_type=F32)


def column_step(fi, halo, own, g, up=None, down=None):
    lane = lanes()
    one = halo[group(g), :]
    two = pltpu.roll(one, 128 - ROWS, 1)
    ka, kb = fields(halo[S:EXT, :])
    a, b = choose(ka, fi[group(g), :]), choose(kb, fi[group(g), :])
    above, below = pltpu.roll(one, 1, 1), pltpu.roll(one, 127, 1)
    if up is not None:
        above = jnp.where(lane == 0, up, above)
        below = jnp.where(lane == ROWS - 1, down, below)
    return a * one + b * ((above + below) + (two + own[group(g), :]))


def interior_kernel(fi, uall, own_w, own_e, halo_w, halo_e, first, f0, f1, f2, s0, s1, s2, acc, col_w, col_e):
    acc[...] = jnp.zeros_like(acc)
    for g in range(GROUPS):
        col_w[group(g), :] = column_step(fi, halo_w, own_w, g)
        col_e[group(g), :] = column_step(fi, halo_e, own_e, g)

    def field(x):
        return lambda t: uall[x, S:EXT, tile(t)]

    def one(x, ref=None, index=None):
        def emit(g, t, p, q):
            first[x, group(g), tile(t)] = p
            first[x, group(g + 1), tile(t)] = q
            if ref is not None:
                split_store(ref, index, g, t, p, q)

        step_row(
            fi,
            field(x),
            lambda g, t: uall[x, group(g), tile(t)],
            lambda g, t: uall[x - 1, group(g), tile(t)],
            lambda g, t: uall[x + 1, group(g), tile(t)],
            lambda g: pltpu.roll(halo_w[group(g), :], (128 - x) % 128, 1),
            lambda g: pltpu.roll(halo_e[group(g), :], 127 - x, 1),
            emit,
        )

    def two(x, ref, index):
        step_row(
            fi,
            field(x),
            lambda g, t: first[x, group(g), tile(t)],
            lambda g, t: first[x - 1, group(g), tile(t)],
            lambda g, t: first[x + 1, group(g), tile(t)],
            lambda g: pltpu.roll(col_w[group(g), :], (128 - x) % 128, 1),
            lambda g: pltpu.roll(col_e[group(g), :], 127 - x, 1),
            lambda g, t, p, q: split_store(ref, index, g, t, p, q),
        )

    one(1)
    one(2, f0, 0)
    one(3, f1, 0)
    two(2, s0, 0)

    def body(i, carry):
        x = 4 + 3 * i
        gram(acc, f0[i], s0[i])
        one(x, f2, i)
        two(x - 1, s1, i)
        gram(acc, f1[i], s1[i])
        one(x + 1, f0, i + 1)
        two(x, s2, i)
        gram(acc, f2[i], s2[i])
        one(x + 2, f1, i + 1)
        two(x + 1, s0, i + 1)
        return carry

    lax.fori_loop(0, THIRD - 1, body, 0)
    end = THIRD - 1
    gram(acc, f0[end], s0[end])
    one(ROWS - 3, f2, end)
    two(ROWS - 4, s1, end)
    gram(acc, f1[end], s1[end])
    one(ROWS - 2)
    two(ROWS - 3, s2, end)
    gram(acc, f2[end], s2[end])


def interior(fi, uall, own_w, own_e, halo_w, halo_e):
    snap = pltpu.VMEM((THIRD, SNAP, COLS), BF16)
    return pl.pallas_call(
        interior_kernel,
        name="interior",
        in_specs=[VM] * 6,
        out_specs=[VM] * 8,
        out_shape=[pltpu.VMEM((ROWS, S, COLS), F32), *[snap] * 6, pltpu.VMEM((SNAP, 2 * SNAP), F32)],
        scratch_shapes=[pltpu.VMEM((S, 128), F32)] * 2,
        cost_estimate=pl.CostEstimate(flops=2 * 12 * SNAP * 2 * SNAP * COLS, bytes_accessed=2**25, transcendentals=0),
        compiler_params=params(8),
    )(fi, uall, own_w, own_e, halo_w, halo_e)


def edge_kernel(
    fi, uall, own_w, own_e, halo_w, halo_e, first, inner, n1, s1, nc, sc, snap_f, snap_s, keep, give, col_w, col_e, edge, acc, packed
):
    acc[...] = inner[...]
    odd = odd_row_device()
    for g in range(GROUPS):
        a, b = nc[group(g), :], sc[group(g), :]
        up, down = jnp.where(odd, a, b), jnp.where(odd, b, a)
        col_w[group(g), :] = column_step(fi, halo_w, own_w, g, up, pltpu.roll(down, ROWS - 1, 1))
        col_e[group(g), :] = column_step(fi, halo_e, own_e, g, pltpu.roll(up, 127, 1), pltpu.roll(down, ROWS - 2, 1))

    def rows(ref, base):
        return lambda g, t: ref[group(g), base + 128 * t : base + 128 * t + 128]

    def at(ref, x):
        return lambda g, t: ref[x, group(g), tile(t)]

    def field(x):
        return lambda t: uall[x, S:EXT, tile(t)]

    def pick(ref, x, to):
        return lambda g: pltpu.roll(ref[group(g), :], (to + 128 - x) & 127, 1)

    for near, corner, at_top in ((n1, nc, odd), (s1, sc, jnp.logical_not(odd))):
        row, inside, deeper = (jnp.where(at_top, i, ROWS - 1 - i) for i in range(3))

        def put(index):
            def emit(g, t, p, q):
                edge[index, group(g), tile(t)] = p
                edge[index, group(g + 1), tile(t)] = q

            return emit

        def put_both(index, target):
            def emit(g, t, p, q):
                put(index)(g, t, p, q)
                split_store(snap_f, target, g, t, p, q)

            return emit

        def put_second(target):
            return lambda g, t, p, q: split_store(snap_s, target, g, t, p, q)

        outer, inner_slot = jnp.where(at_top, 0, 3), jnp.where(at_top, 1, 2)
        step_row(
            fi,
            lambda t, near=near: near[8 * t : 8 * t + 8, FIELD : FIELD + 128],
            rows(near, 0),
            rows(near, COLS),
            at(uall, row),
            pick(corner, 0, 0),
            pick(corner, 1, 127),
            put(0),
        )
        step_row(
            fi, field(row), at(uall, row), rows(near, 0), at(uall, inside),
            pick(halo_w, row, 0), pick(halo_e, row, 127), put_both(1, outer),
        )
        step_row(
            fi, field(row), at(edge, 1), at(edge, 0), at(first, inside),
            pick(col_w, row, 0), pick(col_e, row, 127), put_second(outer),
        )
        step_row(
            fi, field(inside), at(first, inside), at(edge, 1), at(first, deeper),
            pick(col_w, inside, 0), pick(col_e, inside, 127), put_second(inner_slot),
        )
        for t in range(TILES):
            for g in range(0, GROUPS, 2):
                split_store(
                    snap_f, inner_slot, g, t,
                    first[inside, group(g), tile(t)], first[inside, group(g + 1), tile(t)],
                )
        gram(acc, snap_f[outer], snap_s[outer])
        gram(acc, snap_f[inner_slot], snap_s[inner_slot])
    cross = acc[:, SNAP:]
    full = acc[:, :SNAP] + (cross + cross.T)
    top, bottom = full[:S, :], pltpu.roll(full[S:, :], S, 1)
    r = lax.broadcasted_iota(jnp.int32, (S, SNAP), 0)
    c = lax.broadcasted_iota(jnp.int32, (S, SNAP), 1)
    packed[0:S, :] = jnp.where((c < S) & (r > c), bottom, top)
    diag = jnp.sum(jnp.where(r == c, bottom, 0.0), axis=0, keepdims=True)
    packed[S : S + 8, :] = jnp.where(lax.broadcasted_iota(jnp.int32, (8, SNAP), 0) == 0, diag, 0.0)
    packed[S + 8 :, :] = jnp.zeros((8, SNAP), F32)
    second = lax.axis_index("core") == 1
    a, b = packed[:HALF, :], packed[HALF:, :]
    keep[...] = jnp.where(second, b, a)
    give[...] = jnp.where(second, a, b)


def edges(fi, uall, own_w, own_e, halo_w, halo_e, first, inner, n1, s1, nc, sc):
    snap, half = pltpu.VMEM((4, SNAP, COLS), BF16), pltpu.VMEM((HALF, SNAP), F32)
    return pl.pallas_call(
        edge_kernel,
        name="edges",
        in_specs=[VM] * 12,
        out_specs=[VM] * 4,
        out_shape=[snap, snap, half, half],
        scratch_shapes=[
            pltpu.VMEM((S, 128), F32),
            pltpu.VMEM((S, 128), F32),
            pltpu.VMEM((2, S, COLS), F32),
            pltpu.VMEM((SNAP, 2 * SNAP), F32),
            pltpu.VMEM((2 * HALF, SNAP), F32),
        ],
        compiler_params=params(8),
    )(fi, uall, own_w, own_e, halo_w, halo_e, first, inner, n1, s1, nc, sc)


def unpack(packed):
    top, diag = packed[0:S, :], packed[S : S + 1, :]
    r = lax.broadcasted_iota(jnp.int32, (S, SNAP), 0)
    c = lax.broadcasted_iota(jnp.int32, (S, SNAP), 1)
    upper = jnp.where(r <= c, top, 0.0)
    lower = pltpu.roll(jnp.where((r > c) & (c < S), top, 0.0), S, 1)
    on_diag = jnp.where(r == c - S, pltpu.roll(jnp.broadcast_to(diag, (8, SNAP)), S, 1)[0:1, :], 0.0)
    zero = jnp.zeros_like(lower)
    return jnp.concatenate([upper, on_diag], 0) + jnp.concatenate([zero, lower], 0).T


def factor(m, z):
    sub = lax.broadcasted_iota(jnp.int32, (8, 128), 0)
    for k in range(SNAP // BLOCK):
        lo = k * BLOCK
        panel = m[lo : lo + BLOCK, :]
        p = {}
        for i in range(BLOCK):
            for j in range(i, BLOCK):
                p[i, j] = jnp.broadcast_to(panel[i : i + 1, lo + j : lo + j + 1], (8, 128))
        rows = [[jnp.broadcast_to(panel[i : i + 1, tile(h)], (8, 128)) for h in range(2)] for i in range(BLOCK)]
        for j in range(BLOCK):
            r = lax.rsqrt(p[j, j])
            u = {i: p[j, i] * r for i in range(j + 1, BLOCK)}
            for i in range(j + 1, BLOCK):
                for l in range(i, BLOCK):
                    p[i, l] = p[i, l] - u[i] * u[l]
            rows[j] = [v * r for v in rows[j]]
            for i in range(j + 1, BLOCK):
                rows[i] = [v - u[i] * w for v, w in zip(rows[i], rows[j])]
        for part in range(BLOCK // 8):
            for h in range(2):
                v = rows[8 * part][h]
                for i in range(1, 8):
                    v = jnp.where(sub == i, rows[8 * part + i][h], v)
                z[lo + 8 * part : lo + 8 * part + 8, tile(h)] = v
        if lo + BLOCK < SNAP:
            done = z[lo : lo + BLOCK, :]
            high = done.astype(BF16)
            left_over = done - high.astype(F32)
            mid = left_over.astype(BF16)
            low = (left_over - mid.astype(F32)).astype(BF16)
            left = jnp.concatenate([high, high, mid, high, low, mid], 0)[:, :SNAP]
            right = jnp.concatenate([high, mid, high, low, high, mid], 0)
            update = lax.dot_general(left, right, (((0,), (0,)), ((), ())), preferred_element_type=F32)
            m[lo + BLOCK :, :] = m[lo + BLOCK :, :] - update[lo + BLOCK :, :]


def basis_kernel(scale, mine, other, *refs):
    (*snaps, out, tri, m, z, buf, sems) = refs
    r = lax.broadcasted_iota(jnp.int32, (SNAP, SNAP), 0)
    c = lax.broadcasted_iota(jnp.int32, (SNAP, SNAP), 1)
    second = lax.axis_index("core") == 1
    a, b = mine[...], other[...]
    m[:, :SNAP] = unpack(jnp.concatenate([jnp.where(second, b, a), jnp.where(second, a, b)], 0))
    m[:, SNAP:] = jnp.where(r == c, 1.0, 0.0)
    factor(m, z)
    tri[...] = jnp.where(r <= c, z[:, :SNAP], 0.0) * (1.0 / scale)
    w = jnp.where(r >= c, z[:, SNAP:], 0.0) * scale
    top = w.astype(BF16)
    rest = (w - top.astype(F32)).astype(BF16)
    twice = jnp.concatenate([top, top], 1)

    def copy(x):
        return pltpu.make_async_copy(buf.at[x], out.at[:, x, :], sems.at[x])

    def row(x, f, s):
        hi = jnp.concatenate([f[:S, :], s[:S, :]], 0)
        both = jnp.concatenate([hi, f[S:, :], s[S:, :]], 0)
        buf[x] = jnp.dot(twice, both, preferred_element_type=F32) + jnp.dot(rest, hi, preferred_element_type=F32)
        copy(x).start()

    def body(i, carry):
        for k in range(3):
            row(2 + 3 * i + k, snaps[k][i], snaps[3 + k][i])
        return carry

    lax.fori_loop(0, THIRD, body, 0)
    for i, x in enumerate((0, 1, ROWS - 2, ROWS - 1)):
        row(x, snaps[6][i], snaps[7][i])
    for x in range(ROWS):
        copy(x).wait()


def make_basis(scale, mine, other, *snaps):
    def kernel(*refs):
        basis_kernel(scale, *refs)

    return pl.pallas_call(
        kernel,
        name="basis",
        in_specs=[VM] * 10,
        out_specs=[HBM, VM],
        out_shape=[
            jax.ShapeDtypeStruct((SNAP, ROWS, COLS), F32),
            jax.ShapeDtypeStruct((SNAP, SNAP), F32),
        ],
        scratch_shapes=[
            pltpu.VMEM((SNAP, 2 * SNAP), F32),
            pltpu.VMEM((SNAP, 2 * SNAP), F32),
            pltpu.VMEM((ROWS, SNAP, COLS), F32),
            pltpu.SemaphoreType.DMA((ROWS,)),
        ],
        compiler_params=params(16),
    )(mine, other, *snaps)


def spread_sum(value, axis):
    count = lax.axis_size(axis)
    every = lax.all_to_all(jnp.broadcast_to(value[None], (count, *value.shape)), axis, 0, 0)
    parts = [every[i] for i in range(count)]
    while len(parts) > 1:
        parts = [a + b for a, b in zip(parts[::2], parts[1::2], strict=True)]
    return parts[0]


def swap_sum(value, axis, *offsets):
    count = lax.axis_size(axis)
    got = [lax.ppermute(value, axis, [(i, i ^ k) for i in range(count)]) for k in offsets]
    total = value + got[0]
    return total if len(got) == 1 else total + (got[1] + got[2])


def pairs(axis, start):
    lower = range(start, lax.axis_size(axis) - 1, 2)
    return [(i, i + 1) for i in lower] + [(i + 1, i) for i in lower]


def shards(initial, kappa, decay, field_index):
    uall, own_w, own_e, row_a, row_b, col_a, col_b, fi = messages(initial, kappa, decay, field_index)
    near_a, near_b = lax.ppermute(row_a, ROWAXIS, pairs(ROWAXIS, 0)), lax.ppermute(row_b, ROWAXIS, pairs(ROWAXIS, 1))
    col_a, col_b = lax.ppermute(col_a, COLAXIS, pairs(COLAXIS, 0)), lax.ppermute(col_b, COLAXIS, pairs(COLAXIS, 1))
    halo_w, halo_e, corner_a, corner_b = corners(col_a, col_b)
    corner_a = lax.ppermute(corner_a, ROWAXIS, pairs(ROWAXIS, 0))
    corner_b = lax.ppermute(corner_b, ROWAXIS, pairs(ROWAXIS, 1))
    first, *inner_snaps, inner = interior(fi, uall, own_w, own_e, halo_w, halo_e)
    edge_f, edge_s, keep, give = edges(
        fi, uall, own_w, own_e, halo_w, halo_e, first, inner, near_a, near_b, corner_a, corner_b
    )
    swap = [(0, 1), (1, 0)]
    mine = keep + lax.ppermute(give, "core", swap)
    mine = swap_sum(swap_sum(mine, "x", 1, 3, 2), "y", 1, 3, 2)
    mine = swap_sum(swap_sum(mine, "z", 1, 3, 2), "z", 7)
    other = lax.ppermute(mine, "core", swap)
    cells = lax.axis_size(ROWAXIS) * lax.axis_size(COLAXIS) * ROWS * COLS
    return make_basis(math.sqrt(cells), mine, other, *inner_snaps, edge_f, edge_s)


def solution(mesh):
    wide, narrow = mesh.devices.shape
    fine = Mesh(mesh.devices.reshape(wide // 4, 4, narrow // 2, 2), ("z", "x", "y", "core"))
    grid = P(None, ROWAXIS, COLAXIS)
    return jax.shard_map(
        shards,
        mesh=fine,
        in_specs=(grid, grid, P(ROWAXIS, COLAXIS), P()),
        out_specs=(grid, P()),
        check_vma=False,
    )
```

```python
import math

import jax
import jax.numpy as jnp
from jax import lax
from jax.experimental import pallas as pl
from jax.experimental.pallas import tpu as pltpu
from jax.sharding import Mesh, PartitionSpec as P

F32, BF16 = jnp.float32, jnp.bfloat16
S, ROWS, COLS, FIELDS = 64, 16, 1024, 4
SNAP = 2 * S
TILES, GROUPS = COLS // 128, S // 8
EXT = S + 8
KAP, DEC = S, S + FIELDS
HALF = (S + 16) // 2
THIRD = (ROWS - 4) // 3
BLOCK = 16
ROWAXIS, COLAXIS = ("z", "x"), ("y", "core")
FIELD, MESSAGE = 2 * COLS, 2 * COLS + 128
HBM = pl.BlockSpec(memory_space=pltpu.HBM)
VM = pl.BlockSpec(memory_space=pltpu.VMEM)


def params(mib):
    return pltpu.CompilerParams(vmem_limit_bytes=mib * 2**20)


def lanes():
    return lax.broadcasted_iota(jnp.int32, (8, 128), 1)


def tile(t):
    return slice(128 * t, 128 * t + 128)


def group(g):
    return slice(8 * g, 8 * g + 8)


def odd_row_device():
    return (lax.axis_index("x") & 1) == 1


def odd_column_device():
    return lax.axis_index("core") == 1


def message_kernel(u, kap, dec, index, uall, west, east, row_a, row_b, col_a, col_b, fi, sems, scalars, index_sem):
    index_copy = pltpu.make_async_copy(index, scalars, index_sem)
    index_copy.start()
    copies = [
        (
            pltpu.make_async_copy(u.at[:, x, :], uall.at[x, 0:S, :], sems.at[0, x]),
            pltpu.make_async_copy(kap.at[:, x, :], uall.at[x, KAP : KAP + FIELDS, :], sems.at[1, x]),
            pltpu.make_async_copy(dec.at[x : x + 1, :], uall.at[x, DEC : DEC + 1, :], sems.at[2, x]),
        )
        for x in range(ROWS)
    ]
    for copy, _, _ in copies:
        copy.start()
    for x in range(ROWS):
        uall[x, S:EXT, :] = jnp.zeros((8, COLS), F32)
    for _, *small in copies:
        for copy in small:
            copy.start()
    index_copy.wait()
    sub = lax.broadcasted_iota(jnp.int32, (8, 128), 0)
    for g in range(GROUPS):
        v = jnp.full((8, 128), scalars[8 * g], jnp.int32)
        for i in range(1, 8):
            v = jnp.where(sub == i, scalars[8 * g + i], v)
        fi[group(g), :] = v
    lane = lanes()
    w = [jnp.zeros((8, 128), F32) for _ in range(GROUPS + 1)]
    e = [jnp.zeros((8, 128), F32) for _ in range(GROUPS + 1)]
    for x in range(ROWS):
        for copy in copies[x]:
            copy.wait()
        for g in range(GROUPS + 1):
            first, last = uall[x, group(g), tile(0)], uall[x, group(g), tile(TILES - 1)]
            w[g] = jnp.where(lane == x, pltpu.roll(first, x, 1), w[g])
            e[g] = jnp.where(lane == x, pltpu.roll(last, x + 1, 1), e[g])
            if g < GROUPS:
                w[g] = jnp.where(lane == ROWS + x, pltpu.roll(first, ROWS + x - 1, 1), w[g])
                e[g] = jnp.where(lane == ROWS + x, pltpu.roll(last, ROWS + x + 2, 1), e[g])
    odd = odd_column_device()
    for g in range(GROUPS + 1):
        west[group(g), :] = w[g]
        east[group(g), :] = e[g]
        col_a[group(g), :] = jnp.where(odd, w[g], e[g])
        col_b[group(g), :] = jnp.where(odd, e[g], w[g])
    odd = odd_row_device()
    for to, top in ((row_a, odd), (row_b, jnp.logical_not(odd))):
        near, far = jnp.where(top, 0, ROWS - 1), jnp.where(top, 1, ROWS - 2)
        to[:, 0:COLS] = uall[near, 0:S, :]
        to[:, COLS : 2 * COLS] = uall[far, 0:S, :]
        for t in range(TILES):
            to[8 * t : 8 * t + 8, FIELD : FIELD + 128] = uall[near, S:EXT, tile(t)]


def messages(initial, kappa, decay, field_index):
    row, col = pltpu.VMEM((S, MESSAGE), F32), pltpu.VMEM((EXT, 128), F32)
    return pl.pallas_call(
        message_kernel,
        name="messages",
        in_specs=[HBM] * 4,
        out_specs=[VM] * 8,
        out_shape=[
            pltpu.VMEM((ROWS, EXT, COLS), F32), col, col, row, row, col, col, pltpu.VMEM((S, 128), jnp.int32),
        ],
        scratch_shapes=[
            pltpu.SemaphoreType.DMA((3, ROWS)), pltpu.SMEM((S,), jnp.int32), pltpu.SemaphoreType.DMA(()),
        ],
        compiler_params=params(52),
    )(initial, kappa, decay, field_index)


def corner_kernel(first_from, second_from, halo_w, halo_e, first_to, second_to):
    lane = lanes()
    odd, odd_row = odd_column_device(), odd_row_device()
    for g in range(GROUPS + 1):
        a, b = first_from[group(g), :], second_from[group(g), :]
        w, e = jnp.where(odd, a, b), jnp.where(odd, b, a)
        halo_w[group(g), :] = w
        halo_e[group(g), :] = e
        if g < GROUPS:
            top = jnp.where(lane == 0, w, pltpu.roll(e, 1, 1))
            w, e = pltpu.roll(w, 128 - (ROWS - 1), 1), pltpu.roll(e, 128 - (ROWS - 2), 1)
            bottom = jnp.where(lane == 0, w, e)
            first_to[group(g), :] = jnp.where(odd_row, top, bottom)
            second_to[group(g), :] = jnp.where(odd_row, bottom, top)


def corners(first_from, second_from):
    halo, message = pltpu.VMEM((EXT, 128), F32), pltpu.VMEM((S, 128), F32)
    return pl.pallas_call(
        corner_kernel,
        name="corners",
        in_specs=[VM] * 2,
        out_specs=[VM] * 4,
        out_shape=[halo, halo, message, message],
        compiler_params=params(2),
    )(first_from, second_from)


def fields(k):
    b = k * 0.2
    keep = 1.0 - jnp.broadcast_to(k[FIELDS : FIELDS + 1, :], (8, 128))
    return keep - 4.0 * b, b


def choose(k, f):
    return jnp.take_along_axis(k, f, axis=0, mode="promise_in_bounds")


def step_row(fi, load_field, center, above, below, edge_w, edge_e, emit):
    lane = lanes()
    low, high = lane == 0, lane == 127
    from_w = [edge_w(g) for g in range(GROUPS)]
    from_e = [pltpu.roll(center(g, 0), 127, 1) for g in range(GROUPS)]
    for t in range(TILES):
        ka, kb = fields(load_field(t))
        held = None
        for g in range(GROUPS):
            here = center(g, t)
            right = pltpu.roll(here, 1, 1)
            west = jnp.where(low, from_w[g], right)
            from_w[g] = right
            nxt = pltpu.roll(center(g, t + 1), 127, 1) if t + 1 < TILES else edge_e(g)
            east = jnp.where(high, nxt, from_e[g])
            from_e[g] = nxt
            a, b = choose(ka, fi[group(g), :]), choose(kb, fi[group(g), :])
            new = a * here + b * ((above(g, t) + below(g, t)) + (west + east))
            if g % 2 == 0:
                held = new
            else:
                emit(g - 1, t, held, new)


def split_store(ref, index, g, t, first, second):
    both = jnp.concatenate([first, second], 0)
    top = both.astype(BF16)
    ref[index, 8 * g : 8 * g + 16, tile(t)] = top
    ref[index, S + 8 * g : S + 8 * g + 16, tile(t)] = (both - top.astype(F32)).astype(BF16)


def gram(acc, f, s):
    hi = jnp.concatenate([f[:S, :], s[:S, :]], 0)
    rhs = jnp.concatenate([hi, f[S:, :], s[S:, :]], 0)
    acc[...] += lax.dot_general(hi, rhs, (((1,), (1,)), ((), ())), preferred_element_type=F32)


def column_step(fi, halo, own, g, up=None, down=None):
    lane = lanes()
    one = halo[group(g), :]
    two = pltpu.roll(one, 128 - ROWS, 1)
    ka, kb = fields(halo[S:EXT, :])
    a, b = choose(ka, fi[group(g), :]), choose(kb, fi[group(g), :])
    above, below = pltpu.roll(one, 1, 1), pltpu.roll(one, 127, 1)
    if up is not None:
        above = jnp.where(lane == 0, up, above)
        below = jnp.where(lane == ROWS - 1, down, below)
    return a * one + b * ((above + below) + (two + own[group(g), :]))


def interior_kernel(fi, uall, own_w, own_e, halo_w, halo_e, first, f0, f1, f2, s0, s1, s2, acc, col_w, col_e):
    acc[...] = jnp.zeros_like(acc)
    for g in range(GROUPS):
        col_w[group(g), :] = column_step(fi, halo_w, own_w, g)
        col_e[group(g), :] = column_step(fi, halo_e, own_e, g)

    def field(x):
        return lambda t: uall[x, S:EXT, tile(t)]

    def one(x, ref=None, index=None):
        def emit(g, t, p, q):
            first[x, group(g), tile(t)] = p
            first[x, group(g + 1), tile(t)] = q
            if ref is not None:
                split_store(ref, index, g, t, p, q)

        step_row(
            fi,
            field(x),
            lambda g, t: uall[x, group(g), tile(t)],
            lambda g, t: uall[x - 1, group(g), tile(t)],
            lambda g, t: uall[x + 1, group(g), tile(t)],
            lambda g: pltpu.roll(halo_w[group(g), :], (128 - x) % 128, 1),
            lambda g: pltpu.roll(halo_e[group(g), :], 127 - x, 1),
            emit,
        )

    def two(x, ref, index):
        step_row(
            fi,
            field(x),
            lambda g, t: first[x, group(g), tile(t)],
            lambda g, t: first[x - 1, group(g), tile(t)],
            lambda g, t: first[x + 1, group(g), tile(t)],
            lambda g: pltpu.roll(col_w[group(g), :], (128 - x) % 128, 1),
            lambda g: pltpu.roll(col_e[group(g), :], 127 - x, 1),
            lambda g, t, p, q: split_store(ref, index, g, t, p, q),
        )

    one(1)
    one(2, f0, 0)
    one(3, f1, 0)
    two(2, s0, 0)

    def body(i, carry):
        x = 4 + 3 * i
        gram(acc, f0[i], s0[i])
        one(x, f2, i)
        two(x - 1, s1, i)
        gram(acc, f1[i], s1[i])
        one(x + 1, f0, i + 1)
        two(x, s2, i)
        gram(acc, f2[i], s2[i])
        one(x + 2, f1, i + 1)
        two(x + 1, s0, i + 1)
        return carry

    lax.fori_loop(0, THIRD - 1, body, 0)
    end = THIRD - 1
    gram(acc, f0[end], s0[end])
    one(ROWS - 3, f2, end)
    two(ROWS - 4, s1, end)
    gram(acc, f1[end], s1[end])
    one(ROWS - 2)
    two(ROWS - 3, s2, end)
    gram(acc, f2[end], s2[end])


def interior(fi, uall, own_w, own_e, halo_w, halo_e):
    snap = pltpu.VMEM((THIRD, SNAP, COLS), BF16)
    return pl.pallas_call(
        interior_kernel,
        name="interior",
        in_specs=[VM] * 6,
        out_specs=[VM] * 8,
        out_shape=[pltpu.VMEM((ROWS, S, COLS), F32), *[snap] * 6, pltpu.VMEM((SNAP, 2 * SNAP), F32)],
        scratch_shapes=[pltpu.VMEM((S, 128), F32)] * 2,
        cost_estimate=pl.CostEstimate(flops=2 * 12 * SNAP * 2 * SNAP * COLS, bytes_accessed=2**25, transcendentals=0),
        compiler_params=params(8),
    )(fi, uall, own_w, own_e, halo_w, halo_e)


def edge_kernel(
    fi, uall, own_w, own_e, halo_w, halo_e, first, inner, n1, s1, nc, sc, snap_f, snap_s, keep, give, col_w, col_e, edge, acc, packed
):
    acc[...] = inner[...]
    odd = odd_row_device()
    for g in range(GROUPS):
        a, b = nc[group(g), :], sc[group(g), :]
        up, down = jnp.where(odd, a, b), jnp.where(odd, b, a)
        col_w[group(g), :] = column_step(fi, halo_w, own_w, g, up, pltpu.roll(down, ROWS - 1, 1))
        col_e[group(g), :] = column_step(fi, halo_e, own_e, g, pltpu.roll(up, 127, 1), pltpu.roll(down, ROWS - 2, 1))

    def rows(ref, base):
        return lambda g, t: ref[group(g), base + 128 * t : base + 128 * t + 128]

    def at(ref, x):
        return lambda g, t: ref[x, group(g), tile(t)]

    def field(x):
        return lambda t: uall[x, S:EXT, tile(t)]

    def pick(ref, x, to):
        return lambda g: pltpu.roll(ref[group(g), :], (to + 128 - x) & 127, 1)

    for near, corner, at_top in ((n1, nc, odd), (s1, sc, jnp.logical_not(odd))):
        row, inside, deeper = (jnp.where(at_top, i, ROWS - 1 - i) for i in range(3))

        def put(index):
            def emit(g, t, p, q):
                edge[index, group(g), tile(t)] = p
                edge[index, group(g + 1), tile(t)] = q

            return emit

        def put_both(index, target):
            def emit(g, t, p, q):
                put(index)(g, t, p, q)
                split_store(snap_f, target, g, t, p, q)

            return emit

        def put_second(target):
            return lambda g, t, p, q: split_store(snap_s, target, g, t, p, q)

        outer, inner_slot = jnp.where(at_top, 0, 3), jnp.where(at_top, 1, 2)
        step_row(
            fi,
            lambda t, near=near: near[8 * t : 8 * t + 8, FIELD : FIELD + 128],
            rows(near, 0),
            rows(near, COLS),
            at(uall, row),
            pick(corner, 0, 0),
            pick(corner, 1, 127),
            put(0),
        )
        step_row(
            fi, field(row), at(uall, row), rows(near, 0), at(uall, inside),
            pick(halo_w, row, 0), pick(halo_e, row, 127), put_both(1, outer),
        )
        step_row(
            fi, field(row), at(edge, 1), at(edge, 0), at(first, inside),
            pick(col_w, row, 0), pick(col_e, row, 127), put_second(outer),
        )
        step_row(
            fi, field(inside), at(first, inside), at(edge, 1), at(first, deeper),
            pick(col_w, inside, 0), pick(col_e, inside, 127), put_second(inner_slot),
        )
        for t in range(TILES):
            for g in range(0, GROUPS, 2):
                split_store(
                    snap_f, inner_slot, g, t,
                    first[inside, group(g), tile(t)], first[inside, group(g + 1), tile(t)],
                )
        gram(acc, snap_f[outer], snap_s[outer])
        gram(acc, snap_f[inner_slot], snap_s[inner_slot])
    cross = acc[:, SNAP:]
    full = acc[:, :SNAP] + (cross + cross.T)
    top, bottom = full[:S, :], pltpu.roll(full[S:, :], S, 1)
    r = lax.broadcasted_iota(jnp.int32, (S, SNAP), 0)
    c = lax.broadcasted_iota(jnp.int32, (S, SNAP), 1)
    packed[0:S, :] = jnp.where((c < S) & (r > c), bottom, top)
    diag = jnp.sum(jnp.where(r == c, bottom, 0.0), axis=0, keepdims=True)
    packed[S : S + 8, :] = jnp.where(lax.broadcasted_iota(jnp.int32, (8, SNAP), 0) == 0, diag, 0.0)
    packed[S + 8 :, :] = jnp.zeros((8, SNAP), F32)
    second = lax.axis_index("core") == 1
    a, b = packed[:HALF, :], packed[HALF:, :]
    keep[...] = jnp.where(second, b, a)
    give[...] = jnp.where(second, a, b)


def edges(fi, uall, own_w, own_e, halo_w, halo_e, first, inner, n1, s1, nc, sc):
    snap, half = pltpu.VMEM((4, SNAP, COLS), BF16), pltpu.VMEM((HALF, SNAP), F32)
    return pl.pallas_call(
        edge_kernel,
        name="edges",
        in_specs=[VM] * 12,
        out_specs=[VM] * 4,
        out_shape=[snap, snap, half, half],
        scratch_shapes=[
            pltpu.VMEM((S, 128), F32),
            pltpu.VMEM((S, 128), F32),
            pltpu.VMEM((2, S, COLS), F32),
            pltpu.VMEM((SNAP, 2 * SNAP), F32),
            pltpu.VMEM((2 * HALF, SNAP), F32),
        ],
        compiler_params=params(8),
    )(fi, uall, own_w, own_e, halo_w, halo_e, first, inner, n1, s1, nc, sc)


def unpack(packed):
    top, diag = packed[0:S, :], packed[S : S + 1, :]
    r = lax.broadcasted_iota(jnp.int32, (S, SNAP), 0)
    c = lax.broadcasted_iota(jnp.int32, (S, SNAP), 1)
    upper = jnp.where(r <= c, top, 0.0)
    lower = pltpu.roll(jnp.where((r > c) & (c < S), top, 0.0), S, 1)
    on_diag = jnp.where(r == c - S, pltpu.roll(jnp.broadcast_to(diag, (8, SNAP)), S, 1)[0:1, :], 0.0)
    zero = jnp.zeros_like(lower)
    return jnp.concatenate([upper, on_diag], 0) + jnp.concatenate([zero, lower], 0).T


def factor(m, z):
    sub = lax.broadcasted_iota(jnp.int32, (8, 128), 0)
    for k in range(SNAP // BLOCK):
        lo = k * BLOCK
        panel = m[lo : lo + BLOCK, :]
        p = {}
        for i in range(BLOCK):
            for j in range(i, BLOCK):
                p[i, j] = jnp.broadcast_to(panel[i : i + 1, lo + j : lo + j + 1], (8, 128))
        rows = [[jnp.broadcast_to(panel[i : i + 1, tile(h)], (8, 128)) for h in range(2)] for i in range(BLOCK)]
        for j in range(BLOCK):
            r = lax.rsqrt(p[j, j])
            u = {i: p[j, i] * r for i in range(j + 1, BLOCK)}
            for i in range(j + 1, BLOCK):
                for l in range(i, BLOCK):
                    p[i, l] = p[i, l] - u[i] * u[l]
            rows[j] = [v * r for v in rows[j]]
            for i in range(j + 1, BLOCK):
                rows[i] = [v - u[i] * w for v, w in zip(rows[i], rows[j])]
        for part in range(BLOCK // 8):
            for h in range(2):
                v = rows[8 * part][h]
                for i in range(1, 8):
                    v = jnp.where(sub == i, rows[8 * part + i][h], v)
                z[lo + 8 * part : lo + 8 * part + 8, tile(h)] = v
        if lo + BLOCK < SNAP:
            done = z[lo : lo + BLOCK, :]
            high = done.astype(BF16)
            left_over = done - high.astype(F32)
            mid = left_over.astype(BF16)
            low = (left_over - mid.astype(F32)).astype(BF16)
            left = jnp.concatenate([high, high, mid, high, low, mid], 0)[:, :SNAP]
            right = jnp.concatenate([high, mid, high, low, high, mid], 0)
            update = lax.dot_general(left, right, (((0,), (0,)), ((), ())), preferred_element_type=F32)
            m[lo + BLOCK :, :] = m[lo + BLOCK :, :] - update[lo + BLOCK :, :]


def basis_kernel(scale, mine, other, *refs):
    (*snaps, out, tri, m, z, buf, sems) = refs
    r = lax.broadcasted_iota(jnp.int32, (SNAP, SNAP), 0)
    c = lax.broadcasted_iota(jnp.int32, (SNAP, SNAP), 1)
    second = lax.axis_index("core") == 1
    a, b = mine[...], other[...]
    m[:, :SNAP] = unpack(jnp.concatenate([jnp.where(second, b, a), jnp.where(second, a, b)], 0))
    m[:, SNAP:] = jnp.where(r == c, 1.0, 0.0)
    factor(m, z)
    tri[...] = jnp.where(r <= c, z[:, :SNAP], 0.0) * (1.0 / scale)
    w = jnp.where(r >= c, z[:, SNAP:], 0.0) * scale
    top = w.astype(BF16)
    rest = (w - top.astype(F32)).astype(BF16)
    twice = jnp.concatenate([top, top], 1)

    def copy(x):
        return pltpu.make_async_copy(buf.at[x], out.at[:, x, :], sems.at[x])

    def row(x, f, s):
        hi = jnp.concatenate([f[:S, :], s[:S, :]], 0)
        both = jnp.concatenate([hi, f[S:, :], s[S:, :]], 0)
        buf[x] = jnp.dot(twice, both, preferred_element_type=F32) + jnp.dot(rest, hi, preferred_element_type=F32)
        copy(x).start()

    def body(i, carry):
        for k in range(3):
            row(2 + 3 * i + k, snaps[k][i], snaps[3 + k][i])
        return carry

    lax.fori_loop(0, THIRD, body, 0)
    for i, x in enumerate((0, 1, ROWS - 2, ROWS - 1)):
        row(x, snaps[6][i], snaps[7][i])
    for x in range(ROWS):
        copy(x).wait()


def make_basis(scale, mine, other, *snaps):
    def kernel(*refs):
        basis_kernel(scale, *refs)

    return pl.pallas_call(
        kernel,
        name="basis",
        in_specs=[VM] * 10,
        out_specs=[HBM, VM],
        out_shape=[
            jax.ShapeDtypeStruct((SNAP, ROWS, COLS), F32),
            jax.ShapeDtypeStruct((SNAP, SNAP), F32),
        ],
        scratch_shapes=[
            pltpu.VMEM((SNAP, 2 * SNAP), F32),
            pltpu.VMEM((SNAP, 2 * SNAP), F32),
            pltpu.VMEM((ROWS, SNAP, COLS), F32),
            pltpu.SemaphoreType.DMA((ROWS,)),
        ],
        compiler_params=params(16),
    )(mine, other, *snaps)


def spread_sum(value, axis):
    count = lax.axis_size(axis)
    every = lax.all_to_all(jnp.broadcast_to(value[None], (count, *value.shape)), axis, 0, 0)
    parts = [every[i] for i in range(count)]
    while len(parts) > 1:
        parts = [a + b for a, b in zip(parts[::2], parts[1::2], strict=True)]
    return parts[0]


def swap_sum(value, axis, *offsets):
    count = lax.axis_size(axis)
    got = [lax.ppermute(value, axis, [(i, i ^ k) for i in range(count)]) for k in offsets]
    total = value + got[0]
    return total if len(got) == 1 else total + (got[1] + got[2])


def pairs(axis, start):
    lower = range(start, lax.axis_size(axis) - 1, 2)
    return [(i, i + 1) for i in lower] + [(i + 1, i) for i in lower]


def shards(initial, kappa, decay, field_index):
    uall, own_w, own_e, row_a, row_b, col_a, col_b, fi = messages(initial, kappa, decay, field_index)
    near_a, near_b = lax.ppermute(row_a, ROWAXIS, pairs(ROWAXIS, 0)), lax.ppermute(row_b, ROWAXIS, pairs(ROWAXIS, 1))
    col_a, col_b = lax.ppermute(col_a, COLAXIS, pairs(COLAXIS, 0)), lax.ppermute(col_b, COLAXIS, pairs(COLAXIS, 1))
    halo_w, halo_e, corner_a, corner_b = corners(col_a, col_b)
    corner_a = lax.ppermute(corner_a, ROWAXIS, pairs(ROWAXIS, 0))
    corner_b = lax.ppermute(corner_b, ROWAXIS, pairs(ROWAXIS, 1))
    first, *inner_snaps, inner = interior(fi, uall, own_w, own_e, halo_w, halo_e)
    edge_f, edge_s, keep, give = edges(
        fi, uall, own_w, own_e, halo_w, halo_e, first, inner, near_a, near_b, corner_a, corner_b
    )
    swap = [(0, 1), (1, 0)]
    mine = keep + lax.ppermute(give, "core", swap)
    mine = swap_sum(swap_sum(mine, "x", 1, 3, 2), "y", 1, 3, 2)
    mine = swap_sum(swap_sum(mine, "z", 1, 3, 2), "z", 7)
    other = lax.ppermute(mine, "core", swap)
    cells = lax.axis_size(ROWAXIS) * lax.axis_size(COLAXIS) * ROWS * COLS
    return make_basis(math.sqrt(cells), mine, other, *inner_snaps, edge_f, edge_s)


def solution(mesh):
    wide, narrow = mesh.devices.shape
    fine = Mesh(mesh.devices.reshape(wide // 4, 4, narrow // 2, 2), ("z", "x", "y", "core"))
    grid = P(None, ROWAXIS, COLAXIS)
    return jax.shard_map(
        shards,
        mesh=fine,
        in_specs=(grid, grid, P(ROWAXIS, COLAXIS), P()),
        out_specs=(grid, P()),
        check_vma=False,
    )
```
